256 devices in a mesh: outer: 32 (over x_lo, z, core), inner: 8 (over y, x_hi).
Axes of the slice: x: 4 (x_hi: 2, x_lo: 2; x = x_hi * 2 + x_lo), y: 4, z: 8, core: 2. Of those that a mesh axis runs over, the one named last changes fastest.
Arguments:
- query_rows: bfloat16 [65536, 1024], P(('outer', 'inner')), may hold values from -6 to 6
- key_rows: bfloat16 [65536, 1024], P(('outer', 'inner')), may hold values from -6 to 6
- value_rows: bfloat16 [65536, 1024], P(('outer', 'inner')), may hold values from -6 to 6
- layer_output: bfloat16 [65536, 1024], P(('outer', 'inner')), may hold values from -1.5 to 1.5
- output_grad: bfloat16 [65536, 1024], P(('outer', 'inner')), may hold values from -192 to 192
- log_norms: float32 [16, 65536], P(None, ('outer', 'inner')), as said below
Outputs:
- query_grad: bfloat16 [65536, 1024], P(('outer', 'inner'))
- key_grad: bfloat16 [65536, 1024], P(('outer', 'inner'))
- value_grad: bfloat16 [65536, 1024], P(('outer', 'inner'))
The draws below stay inside these ranges and needn't reach their ends.
Inputs may be any that keep to these rules, and one draw needn't show every extreme that they name: `log_norms`: every entry lies within 1 of log(1280) + 0.5.
All inputs are finite; a program needn't handle non-finite values.
Results may differ from the reference program's by a relative error of at most 0.0057.
Values may be sent and summed in bfloat16 or wider, within the bound.
No kernel may reach another device: no remote copies, remote signals or barrier semaphores. Data moves between devices by JAX's collectives and lax.ppermute only.
A program may use at most 128 MiB of HBM per device.

```python
import math
import jax
import jax.numpy as jnp
from jax import lax

HEADS = 16
HEAD_DIM = 64
REACH = 2
TOK_DEV = 256
D = 1024
TOKENS = 65536


def draw_log_norms(key, part):
    key = jax.random.fold_in(key, 11)
    center = math.log(TOK_DEV * (2 * REACH + 1)) + 0.5
    offset = jax.random.uniform(key, (HEADS, TOKENS), jnp.float32, -1.0, 1.0)
    return center + offset


def block_scale(stream_key, extent, split, smallest, top_value):
    level = 1.0
    for axis_at, parts in split:
        steps = jax.random.uniform(jax.random.fold_in(jax.random.fold_in(stream_key, 6), axis_at), (parts,), jnp.float32, smallest / len(split), top_value / len(split))
        level = level * jnp.repeat(jnp.exp(steps), extent[axis_at] // parts).reshape((-1,) + (1,) * (len(extent) - 1 - axis_at))
    return level


def noise(rng, shape, width, most, cuts=(), held_as=jnp.bfloat16):
    entries = width * jax.random.normal(rng, shape, jnp.float32)
    if cuts:
        entries = entries * block_scale(rng, shape, cuts, -0.22, 0.18)
    return jnp.clip(entries, -most, most).astype(held_as)


def setup_inputs(seed: int = 0) -> dict:
    seeds = jax.random.split(jax.random.key(seed), 7)
    query_rows = noise(seeds[0], (TOKENS, D), 1.0, 6.0, ((0, 256),))
    key_rows = noise(seeds[1], (TOKENS, D), 1.0, 6.0, ((0, 256),))
    value_rows = noise(seeds[2], (TOKENS, D), 1.0, 6.0, ((0, 256),))
    layer_output = noise(seeds[3], (TOKENS, D), 0.25, 1.5, ((0, 256),))
    output_grad = noise(seeds[4], (TOKENS, D), 32.0, 192.0, ((0, 256),))
    log_norms = draw_log_norms(jax.random.fold_in(seeds[6], 71), 0)
    return dict(query_rows=query_rows, key_rows=key_rows, value_rows=value_rows, layer_output=layer_output, output_grad=output_grad, log_norms=log_norms)


def reference(query_rows, key_rows, value_rows, layer_output, output_grad, log_norms):
    tok_rows = TOK_DEV
    span_rows = (2 * REACH + 1) * TOK_DEV
    block_count = TOKENS // TOK_DEV
    model_width = HEADS * HEAD_DIM
    scale = HEAD_DIM ** -0.5
    products = layer_output.astype(jnp.float32) * output_grad.astype(jnp.float32)
    row_delta = products.reshape(TOKENS, HEADS, HEAD_DIM).sum(-1).T
    margin = jnp.zeros((REACH * tok_rows, model_width), jnp.bfloat16)
    key_padded = jnp.concatenate([margin, key_rows, margin], axis=0)
    value_padded = jnp.concatenate([margin, value_rows, margin], axis=0)

    def visit(carry, block):
        key_acc, value_acc = carry
        start = (block * tok_rows).astype(jnp.int32)
        query_block = lax.dynamic_slice_in_dim(query_rows, start, tok_rows, 0).astype(jnp.float32).reshape(tok_rows, HEADS, HEAD_DIM)
        grad_block = lax.dynamic_slice_in_dim(output_grad, start, tok_rows, 0).astype(jnp.float32).reshape(tok_rows, HEADS, HEAD_DIM)
        key_window = lax.dynamic_slice_in_dim(key_padded, start, span_rows, 0).astype(jnp.float32).reshape(span_rows, HEADS, HEAD_DIM)
        value_window = lax.dynamic_slice_in_dim(value_padded, start, span_rows, 0).astype(jnp.float32).reshape(span_rows, HEADS, HEAD_DIM)
        norm_block = lax.dynamic_slice_in_dim(log_norms, start, tok_rows, 1)
        delta_block = lax.dynamic_slice_in_dim(row_delta, start, tok_rows, 1)
        key_block_index = block - REACH + jnp.arange(span_rows, dtype=jnp.int32) // tok_rows
        present = ((key_block_index >= 0) & (key_block_index < block_count)).astype(jnp.float32)
        scores = jnp.einsum("qhe,khe->hqk", query_block, key_window) * scale
        probs = jnp.exp(scores - norm_block[:, :, None]) * present[None, None, :]
        weights = lax.optimization_barrier(probs.astype(jnp.bfloat16)).astype(jnp.float32)
        grad_value = jnp.einsum("hqk,qhe->khe", weights, grad_block).reshape(span_rows, model_width)
        grad_prob = jnp.einsum("qhe,khe->hqk", grad_block, value_window)
        grad_score = lax.optimization_barrier((probs * (grad_prob - delta_block[:, :, None])).astype(jnp.bfloat16)).astype(jnp.float32)
        grad_query = jnp.einsum("hqk,khe->qhe", grad_score, key_window).reshape(tok_rows, model_width)
        grad_key = jnp.einsum("hqk,qhe->khe", grad_score, query_block).reshape(span_rows, model_width)
        key_acc = lax.dynamic_update_slice_in_dim(key_acc, lax.dynamic_slice_in_dim(key_acc, start, span_rows, 0) + grad_key, start, 0)
        value_acc = lax.dynamic_update_slice_in_dim(value_acc, lax.dynamic_slice_in_dim(value_acc, start, span_rows, 0) + grad_value, start, 0)
        return (key_acc, value_acc), grad_query

    empty = jnp.zeros(((block_count + 2 * REACH) * tok_rows, model_width), jnp.float32)
    (key_acc, value_acc), query_parts = lax.scan(visit, (empty, empty), jnp.arange(block_count, dtype=jnp.int32))
    first = REACH * tok_rows
    query_grad = (query_parts.reshape(TOKENS, model_width) * scale).astype(jnp.bfloat16)
    key_grad = (key_acc[first:first + TOKENS] * scale).astype(jnp.bfloat16)
    value_grad = value_acc[first:first + TOKENS].astype(jnp.bfloat16)
    return query_grad, key_grad, value_grad
```

```python
import functools

import jax
import jax.numpy as jnp
from jax import lax
from jax.experimental import pallas as pl
from jax.experimental.pallas import tpu as pltpu
from jax.sharding import PartitionSpec as P

AXES = ("outer", "inner")
LANES = 128
LOG2E = 1.4426950408889634
VMEM_LIMIT = 48 * 1024 * 1024


def params():
    return pltpu.CompilerParams(
        dimension_semantics=("arbitrary",), vmem_limit_bytes=VMEM_LIMIT
    )


def dot_nt(a, b):
    return lax.dot_general(a, b, (((1,), (1,)), ((), ())), preferred_element_type=jnp.float32)


def dot_nn(a, b):
    return lax.dot_general(a, b, (((1,), (0,)), ((), ())), preferred_element_type=jnp.float32)


def head_masks(dtype):
    lane = lax.broadcasted_iota(jnp.int32, (1, LANES), 1)
    first = jnp.where(lane < LANES // 2, 1.0, 0.0)
    return first.astype(dtype), (1.0 - first).astype(dtype)


def pack_kernel(x_ref, *refs):
    rows = refs[0].shape[0]
    norm_ref = refs[10]
    step = pl.program_id(0)
    for side in range(2):
        q, k, v, o, g = refs[5 * side : 5 * side + 5]
        msg, kv = refs[11 + 2 * side : 13 + 2 * side]
        half = x_ref[0] if side == 0 else 1 - x_ref[0]
        pair = half * pl.num_programs(0) + step
        grad = g[...]
        msg[0:rows] = q[...]
        msg[rows : 2 * rows] = grad
        kv[0:rows] = k[...]
        kv[rows : 2 * rows] = v[...]
        product = o[...].astype(jnp.float32) * grad.astype(jnp.float32)
        high = product.astype(jnp.bfloat16)
        low = (product - high.astype(jnp.float32)).astype(jnp.bfloat16)
        row = lax.broadcasted_iota(jnp.int32, (8, LANES), 0)
        lane = lax.broadcasted_iota(jnp.int32, (8, LANES), 1)
        pick = jnp.where(row == lane // (LANES // 2), 1.0, 0.0).astype(jnp.bfloat16)
        delta = dot_nt(pick, high) + dot_nt(pick, low)
        norms = [norm_ref[pl.ds(2 * pair + h, 1), :] for h in range(2)]
        terms = jnp.concatenate([*norms, delta[0:2]], axis=0)
        terms_high = terms.astype(jnp.bfloat16).astype(jnp.float32)
        both = jnp.concatenate([terms_high, terms - terms_high], axis=0)
        msg[2 * rows : 2 * rows + 16] = jnp.concatenate(
            [both[:, :LANES], both[:, LANES:]], axis=0
        ).astype(jnp.bfloat16)


def pack(x, q, k, v, o, g, norms):
    rows, width = q.shape
    pairs = width // LANES // 2
    own = pl.BlockSpec((rows, LANES), lambda i, x: (0, x[0] * pairs + i))
    other = pl.BlockSpec((rows, LANES), lambda i, x: (0, (1 - x[0]) * pairs + i))
    msg_spec = pl.BlockSpec((2 * rows + 16, LANES), lambda i, x: (0, i))
    kv_spec = pl.BlockSpec((2 * rows, LANES), lambda i, x: (0, i))
    msg = jax.ShapeDtypeStruct((2 * rows + 16, width // 2), jnp.bfloat16)
    kv = jax.ShapeDtypeStruct((2 * rows, width // 2), jnp.bfloat16)
    return pl.pallas_call(
        pack_kernel,
        grid_spec=pltpu.PrefetchScalarGridSpec(
            num_scalar_prefetch=1,
            grid=(pairs,),
            in_specs=[own] * 5
            + [other] * 5
            + [pl.BlockSpec(norms.shape, lambda i, x: (0, 0))],
            out_specs=[msg_spec, kv_spec, msg_spec, kv_spec],
        ),
        out_shape=[msg, kv, msg, kv],
        compiler_params=params(),
        name="pack",
    )(x, q, k, v, o, g, q, k, v, o, g, norms)


def tiles_kernel(*refs, keys, queries, pairs, dq_in, dkv_in, dq_out, scale):
    refs = list(refs)
    kv_refs = {u: refs.pop(0) for u in keys}
    msg_refs = {t: refs.pop(0) for t in queries}
    dq = {t: refs.pop(0)[...] for t in dq_in}
    dkv_refs = {u: refs.pop(0) for u in dkv_in}
    dq_refs = {t: refs.pop(0) for t in dq_out}
    dkv_out = {u: refs.pop(0) for u in keys}
    rows = next(iter(kv_refs.values())).shape[0] // 2
    masks = head_masks(jnp.bfloat16)
    loaded = {}
    for t in queries:
        msg = msg_refs[t]
        q, g = msg[0:rows], msg[rows : 2 * rows]
        info = msg[2 * rows : 2 * rows + 16].astype(jnp.float32)
        both = jnp.concatenate([info[0:8], info[8:16]], axis=1)
        terms = both[0:4] + both[4:8]
        loaded[t] = ([q * m for m in masks], [g * m for m in masks], terms[0:2] * LOG2E, terms[2:4])
    acc = {t: [None, None] for t in queries}
    for u in keys:
        k, v = kv_refs[u][0:rows], kv_refs[u][rows : 2 * rows]
        kt = k.T
        half = LANES // 2
        heads_t = [kt[0:half], kt[half:LANES]]
        dk = dkv_refs[u][0:rows] if u in dkv_refs else None
        dv = dkv_refs[u][rows : 2 * rows] if u in dkv_refs else None
        for t in queries:
            if (u, t) not in pairs:
                continue
            qs, gs, norms, deltas = loaded[t]
            for h in range(2):
                scores = dot_nt(k, qs[h])
                probs = jnp.exp2(scores * (scale * LOG2E) - norms[h : h + 1])
                grad_prob = dot_nt(v, gs[h])
                grad_score = (probs * (grad_prob - deltas[h : h + 1])).astype(jnp.bfloat16)
                weights = probs.astype(jnp.bfloat16)
                part = dot_nn(weights, gs[h])
                dv = part if dv is None else dv + part
                part = dot_nn(grad_score, qs[h])
                dk = part if dk is None else dk + part
                part = dot_nn(heads_t[h], grad_score)
                acc[t][h] = part if acc[t][h] is None else acc[t][h] + part
        final = dkv_out[u].dtype == jnp.bfloat16
        dkv_out[u][0:rows] = (dk * scale if final else dk).astype(dkv_out[u].dtype)
        dkv_out[u][rows : 2 * rows] = dv.astype(dkv_out[u].dtype)
    for t in queries:
        total = jnp.concatenate(acc[t], axis=0).T
        if t in dq:
            total = total + dq[t]
        final = dq_refs[t].dtype == jnp.bfloat16
        dq_refs[t][...] = (total * scale if final else total).astype(dq_refs[t].dtype)


def tiles(kvs, msgs, pairs, dq_in, dkv_in, dq_types, dkv_types, scale, name):
    first = next(iter(kvs.values()))
    rows, width = first.shape[0] // 2, first.shape[1]

    def spec(height):
        return pl.BlockSpec((height, LANES), lambda i: (0, i))

    operands = [*kvs.values(), *msgs.values(), *dq_in.values(), *dkv_in.values()]
    outs = [jax.ShapeDtypeStruct((rows, width), dq_types[t]) for t in msgs]
    outs += [jax.ShapeDtypeStruct((2 * rows, width), dkv_types[u]) for u in kvs]
    results = pl.pallas_call(
        functools.partial(
            tiles_kernel,
            keys=tuple(kvs),
            queries=tuple(msgs),
            pairs=frozenset(pairs),
            dq_in=tuple(dq_in),
            dkv_in=tuple(dkv_in),
            dq_out=tuple(msgs),
            scale=scale,
        ),
        grid=(width // LANES,),
        in_specs=[spec(a.shape[0]) for a in operands],
        out_specs=[spec(a.shape[0]) for a in outs],
        out_shape=outs,
        compiler_params=params(),
        name=name,
    )(*operands)
    count = len(msgs)
    return dict(zip(msgs, results[:count])), dict(zip(kvs, results[count:]))


def finish_kernel(x_ref, dq_own, ret_a, ret_b, dkv_own, dq_other, dkv_other, dq, dk, dv, *, scale):
    rows = dq.shape[0]
    own = pl.program_id(0) < pl.num_programs(0) // 2

    @pl.when(own)
    def _():
        total = dq_own[...] * scale + ret_a[...].astype(jnp.float32) + ret_b[...].astype(jnp.float32)
        dq[...] = total.astype(jnp.bfloat16)
        dk[...] = dkv_own[0:rows]
        dv[...] = dkv_own[rows : 2 * rows]

    @pl.when(jnp.logical_not(own))
    def _():
        dq[...] = dq_other[...]
        dk[...] = dkv_other[0:rows]
        dv[...] = dkv_other[rows : 2 * rows]


def finish(x, dq_own, ret_a, ret_b, dkv_own, dq_other, dkv_other, scale):
    rows, width = dq_own.shape
    pairs = width // LANES

    def own_spec(height):
        return pl.BlockSpec((height, LANES), lambda i, x: (0, jnp.minimum(i, pairs - 1)))

    def other_spec(height):
        return pl.BlockSpec((height, LANES), lambda i, x: (0, jnp.maximum(i - pairs, 0)))

    out = pl.BlockSpec((rows, LANES), lambda i, x: (0, (x[0] * pairs + i) % (2 * pairs)))
    return pl.pallas_call(
        functools.partial(finish_kernel, scale=scale),
        grid_spec=pltpu.PrefetchScalarGridSpec(
            num_scalar_prefetch=1,
            grid=(2 * pairs,),
            in_specs=[own_spec(rows)] * 3
            + [own_spec(2 * rows), other_spec(rows), other_spec(2 * rows)],
            out_specs=[out] * 3,
        ),
        out_shape=[jax.ShapeDtypeStruct((rows, 2 * width), jnp.bfloat16)] * 3,
        compiler_params=params(),
        name="finish",
    )(x, dq_own, ret_a, ret_b, dkv_own, dq_other, dkv_other)


def per_device(query_rows, key_rows, value_rows, layer_output, output_grad, log_norms):
    count = lax.axis_size("outer") * lax.axis_size("inner")
    index = lax.axis_index("outer") * lax.axis_size("inner") + lax.axis_index("inner")
    x = (index % 2).astype(jnp.int32).reshape(1)
    head_size = query_rows.shape[1] // log_norms.shape[0]
    scale = head_size ** (-0.5)

    swap = [(i, i ^ 1) for i in range(count)]
    step_a = [(i, i + 2 if i % 2 == 0 else i - 2) for i in range(count)]
    step_a = [(i, j) for i, j in step_a if 0 <= j < count]
    step_b = [(j, i) for i, j in step_a]

    def send(a, perm):
        return lax.ppermute(a, AXES, perm)

    own, kv_own, to_other, kv_to_other = pack(
        x, query_rows, key_rows, value_rows, layer_output, output_grad, log_norms
    )
    other = send(to_other, swap)
    near_a, near_b = send(own, step_a), send(own, step_b)
    kv_to_other, other = lax.optimization_barrier((kv_to_other, other))
    far_a, far_b = send(other, step_a), send(other, step_b)
    kv_other = send(kv_to_other, swap)

    f32, b16 = jnp.float32, jnp.bfloat16
    dq1, dkv1 = tiles(
        {"own": kv_own},
        {"own": own, "other": other, "near_a": near_a, "near_b": near_b},
        [("own", t) for t in ("own", "other", "near_a", "near_b")],
        {},
        {},
        {"own": f32, "other": f32, "near_a": b16, "near_b": f32},
        {"own": f32},
        scale,
        "tiles_near",
    )
    dq2, dkv2 = tiles(
        {"other": kv_other, "own": kv_own},
        {"own": own, "other": other, "near_b": near_b, "far_a": far_a, "far_b": far_b},
        [("other", t) for t in ("own", "other", "near_b", "far_a", "far_b")] + [("own", "far_a")],
        {t: dq1[t] for t in ("own", "other", "near_b")},
        {"own": dkv1["own"]},
        {"own": f32, "other": f32, "near_b": b16, "far_a": b16, "far_b": b16},
        {"other": b16, "own": b16},
        scale,
        "tiles_far",
    )
    back_far_a, back_far_b = send(dq2["far_a"], step_b), send(dq2["far_b"], step_a)
    dkv_other = send(dkv2["other"], swap)
    back_near_a, back_near_b = send(dq1["near_a"], step_b), send(dq2["near_b"], step_a)
    dq_other = (
        dq2["other"] * scale + back_far_a.astype(jnp.float32) + back_far_b.astype(jnp.float32)
    ).astype(jnp.bfloat16)
    dq_other = send(dq_other, swap)
    return tuple(
        finish(x, dq2["own"], back_near_a, back_near_b, dkv2["own"], dq_other, dkv_other, scale)
    )


def solution(mesh):
    rows = P(AXES, None)
    return jax.shard_map(
        per_device,
        mesh=mesh,
        in_specs=(rows, rows, rows, rows, rows, P(None, AXES)),
        out_specs=(rows, rows, rows),
        check_vma=False,
    )
```

```python
import functools

import jax
import jax.numpy as jnp
from jax import lax
from jax.experimental import pallas as pl
from jax.experimental.pallas import tpu as pltpu
from jax.sharding import PartitionSpec as P

AXES = ("outer", "inner")
LANES = 128
LOG2E = 1.4426950408889634
WHOLE = pl.BlockSpec(memory_space=pltpu.VMEM)
IN_HBM = pl.BlockSpec(memory_space=pltpu.HBM)
PARAMS = pltpu.CompilerParams(vmem_limit_bytes=16 * 1024 * 1024)


def dot_nt(a, b):
    return lax.dot_general(a, b, (((1,), (1,)), ((), ())), preferred_element_type=jnp.float32)


def dot_nn(a, b):
    return lax.dot_general(a, b, (((1,), (0,)), ((), ())), preferred_element_type=jnp.float32)


def head_masks(dtype):
    lane = lax.broadcasted_iota(jnp.int32, (1, LANES), 1)
    first = jnp.where(lane < LANES // 2, 1.0, 0.0)
    return first.astype(dtype), (1.0 - first).astype(dtype)


def pack_kernel(x_ref, q, k, v, o, g, norms, msg, kv, msg_other, kv_other, outs, norm_buf, sems, norm_sem):
    rows, width = q.shape
    half = width // 2
    sides = ((1 - x_ref[0], msg_other, kv_other), (x_ref[0], msg, kv))
    norm_copy = pltpu.make_async_copy(norms, norm_buf, norm_sem)
    norm_copy.start()
    copies = []
    for at, (side, to, _) in enumerate(sides):
        columns = pl.ds(pl.multiple_of(side * half, LANES), half)
        moves = ((g, to.at[rows : 2 * rows]), (o, outs.at[at]), (q, to.at[0:rows]))
        copies.append([pltpu.make_async_copy(a.at[:, columns], b, sems.at[at, n]) for n, (a, b) in enumerate(moves)])
    later = []
    for at, (side, _, to) in enumerate(sides):
        columns = pl.ds(pl.multiple_of(side * half, LANES), half)
        moves = ((k, to.at[0:rows]), (v, to.at[rows : 2 * rows]))
        later += [pltpu.make_async_copy(a.at[:, columns], b, sems.at[at, 3 + n]) for n, (a, b) in enumerate(moves)]
    for copy in copies[0] + copies[1] + later:
        copy.start()
    norm_copy.wait()
    row = lax.broadcasted_iota(jnp.int32, (8, LANES), 0)
    lane = lax.broadcasted_iota(jnp.int32, (8, LANES), 1)
    pick = jnp.where(row == lane // (LANES // 2), 1.0, 0.0).astype(jnp.bfloat16)
    for at, (side, to, _) in enumerate(sides):
        copies[at][0].wait()
        copies[at][1].wait()
        for pair in range(half // LANES):
            span = slice(pair * LANES, (pair + 1) * LANES)
            product = outs[at, :, span].astype(jnp.float32) * to[rows : 2 * rows, span].astype(jnp.float32)
            high = product.astype(jnp.bfloat16)
            low = (product - high.astype(jnp.float32)).astype(jnp.bfloat16)
            delta = dot_nt(pick, high) + dot_nt(pick, low)
            first = 2 * (side * (half // LANES) + pair)
            terms = jnp.concatenate(
                [norm_buf[pl.ds(first, 1), :], norm_buf[pl.ds(first + 1, 1), :], delta[0:2]], axis=0
            )
            terms_high = terms.astype(jnp.bfloat16).astype(jnp.float32)
            both = jnp.concatenate([terms_high, terms - terms_high], axis=0)
            to[2 * rows : 2 * rows + 16, span] = jnp.concatenate(
                [both[:, :LANES], both[:, LANES:]], axis=0
            ).astype(jnp.bfloat16)
        copies[at][2].wait()
    for copy in later:
        copy.wait()


def pack(x, q, k, v, o, g, norms):
    rows, width = q.shape
    msg = jax.ShapeDtypeStruct((2 * rows + 16, width // 2), jnp.bfloat16)
    kv = jax.ShapeDtypeStruct((2 * rows, width // 2), jnp.bfloat16)
    return pl.pallas_call(
        pack_kernel,
        in_specs=[pl.BlockSpec(memory_space=pltpu.SMEM)] + [IN_HBM] * 6,
        out_specs=[WHOLE] * 4,
        out_shape=[msg, kv, msg, kv],
        scratch_shapes=[
            pltpu.VMEM((2, rows, width // 2), jnp.bfloat16),
            pltpu.VMEM(norms.shape, jnp.float32),
            pltpu.SemaphoreType.DMA((2, 5)),
            pltpu.SemaphoreType.DMA,
        ],
        compiler_params=PARAMS,
        name="pack",
    )(x, *(pltpu.with_memory_space_constraint(a, pltpu.HBM) for a in (q, k, v, o, g, norms)))


def run_tiles(kv_refs, msg_refs, pairs, dq_in, dkv_in, dq_out, dkv_out, scale):
    rows, width = next(iter(kv_refs.values())).shape
    rows //= 2
    half = LANES // 2
    masks = head_masks(jnp.bfloat16)
    key_side, query_side = {}, {}

    def span(group):
        return slice(group * LANES, (group + 1) * LANES)

    def keys_of(u, group):
        if (u, group) not in key_side:
            k, v = kv_refs[u][0:rows, span(group)], kv_refs[u][rows : 2 * rows, span(group)]
            kt = k.T
            sums = [None, None]
            if u in dkv_in:
                sums = [dkv_in[u][0:rows, span(group)], dkv_in[u][rows : 2 * rows, span(group)]]
            key_side[u, group] = (k, v, [kt[0:half], kt[half:LANES]], sums)
        return key_side[u, group]

    def queries_of(t, group):
        if (t, group) not in query_side:
            msg = msg_refs[t]
            q, g = msg[0:rows, span(group)], msg[rows : 2 * rows, span(group)]
            info = msg[2 * rows : 2 * rows + 16, span(group)].astype(jnp.float32)
            both = jnp.concatenate([info[0:8], info[8:16]], axis=1)
            terms = both[0:4] + both[4:8]
            query_side[t, group] = (
                [q * m for m in masks],
                [g * m for m in masks],
                terms[0:2] * LOG2E,
                terms[2:4],
                [None, None],
            )
        return query_side[t, group]

    def plus(a, b):
        return b if a is None else a + b

    items = [(group, u, t, h) for group in range(width // LANES) for u, t in pairs for h in range(2)]
    last_of = {}
    for group, u, t, h in items:
        last_of["key", u, group] = last_of["query", t, group] = (group, u, t, h)

    def products(item):
        group, u, t, h = item
        k, v, _, _ = keys_of(u, group)
        qs, gs = queries_of(t, group)[:2]
        return dot_nt(k, qs[h]), dot_nt(v, gs[h])

    def weigh(item, scores, grad_prob):
        group, u, t, h = item
        _, _, norms, deltas, _ = queries_of(t, group)
        probs = jnp.exp2(scores * (scale * LOG2E) - norms[h : h + 1])
        grad_score = probs * (grad_prob - deltas[h : h + 1])
        return probs.astype(jnp.bfloat16), grad_score.astype(jnp.bfloat16)

    def add_up(item, weights, grad_score):
        group, u, t, h = item
        _, _, kt, sums = keys_of(u, group)
        qs, gs, _, _, dq = queries_of(t, group)
        sums[1] = plus(sums[1], dot_nn(weights, gs[h]))
        sums[0] = plus(sums[0], dot_nn(grad_score, qs[h]))
        dq[h] = plus(dq[h], dot_nn(kt[h], grad_score))
        if last_of["query", t, group] == item:
            total = jnp.concatenate(dq, axis=0).T
            if t in dq_in:
                total = total + dq_in[t][:, span(group)]
            ref = dq_out[t]
            final = ref.dtype == jnp.bfloat16
            ref[:, span(group)] = (total * scale if final else total).astype(ref.dtype)
        if last_of["key", u, group] == item:
            ref = dkv_out[u]
            final = ref.dtype == jnp.bfloat16
            ref[0:rows, span(group)] = (sums[0] * scale if final else sums[0]).astype(ref.dtype)
            ref[rows : 2 * rows, span(group)] = sums[1].astype(ref.dtype)

    made, weighed = {}, {}
    for step in range(len(items) + 2):
        if step < len(items):
            made[step] = products(items[step])
        if 0 <= step - 1 < len(items):
            weighed[step - 1] = weigh(items[step - 1], *made.pop(step - 1))
        if 0 <= step - 2:
            add_up(items[step - 2], *weighed.pop(step - 2))


def near_kernel(kv, own, other, near_1, near_2, dq_own, dq_other, dq_1, dq_2, dkv, *, scale):
    run_tiles(
        {"own": kv},
        {"own": own, "other": other, "1": near_1, "2": near_2},
        [("own", t) for t in ("own", "1", "2", "other")],
        {},
        {},
        {"own": dq_own, "other": dq_other, "1": dq_1, "2": dq_2},
        {"own": dkv},
        scale,
    )


def near_tiles(kv, own, other, near_1, near_2, scale):
    rows, width = kv.shape[0] // 2, kv.shape[1]
    part = jax.ShapeDtypeStruct((rows, width), jnp.float32)
    return pl.pallas_call(
        functools.partial(near_kernel, scale=scale),
        in_specs=[WHOLE] * 5,
        out_specs=[WHOLE] * 5,
        out_shape=[part] * 4 + [jax.ShapeDtypeStruct(kv.shape, jnp.float32)],
        compiler_params=PARAMS,
        name="near_tiles",
    )(kv, own, other, near_1, near_2)


def far_kernel(
    place_ref, kv, kv_other, own, other, near_1, near_2, far_1, far_2, dq_own, dq_other, dq_1, dq_2, dkv,
    out_own, out_other, back_1, back_2, dkv_own, dkv_other, near_b, far_a, far_b, dq_b, back_a, back_b, *, scale
):
    rows = dq_1.shape[0]

    def sort(sides):
        (near_a_in, far_a_in, dq_a_in), (near_b_in, far_b_in, dq_b_in) = sides
        near_b[...] = near_b_in[...]
        far_a[...] = far_a_in[...]
        far_b[...] = far_b_in[...]
        dq_b[...] = dq_b_in[...]
        back_a[0:rows] = (dq_a_in[...] * scale).astype(back_a.dtype)

    first, second = (near_1, far_1, dq_1), (near_2, far_2, dq_2)
    pl.when(place_ref[1] == 1)(lambda: sort((first, second)))
    pl.when(place_ref[1] != 1)(lambda: sort((second, first)))
    run_tiles(
        {"own": kv, "other": kv_other},
        {"own": own, "other": other, "near_b": near_b, "far_a": far_a, "far_b": far_b},
        [("other", "near_b"), ("other", "far_b"), ("other", "far_a"), ("own", "far_a"), ("other", "own"), ("other", "other")],
        {"own": dq_own, "other": dq_other, "near_b": dq_b},
        {"own": dkv},
        {
            "own": out_own,
            "other": out_other,
            "near_b": back_b.at[0:rows],
            "far_a": back_a.at[rows : 2 * rows],
            "far_b": back_b.at[rows : 2 * rows],
        },
        {"own": dkv_own, "other": dkv_other},
        scale,
    )

    def unsort(out_a, out_b):
        out_a[...] = back_a[...]
        out_b[...] = back_b[...]

    pl.when(place_ref[1] == 1)(lambda: unsort(back_1, back_2))
    pl.when(place_ref[1] != 1)(lambda: unsort(back_2, back_1))


def far_tiles(x, *operands, scale):
    kv, msg = operands[0], operands[2]
    rows, width = kv.shape[0] // 2, kv.shape[1]
    part = jax.ShapeDtypeStruct((rows, width), jnp.float32)
    done = jax.ShapeDtypeStruct(kv.shape, jnp.bfloat16)
    return pl.pallas_call(
        functools.partial(far_kernel, scale=scale),
        in_specs=[pl.BlockSpec(memory_space=pltpu.SMEM)] + [WHOLE] * len(operands),
        out_specs=[WHOLE] * 6,
        out_shape=[part, part] + [done] * 4,
        scratch_shapes=[pltpu.VMEM(msg.shape, msg.dtype)] * 3
        + [pltpu.VMEM(part.shape, part.dtype)]
        + [pltpu.VMEM(done.shape, done.dtype)] * 2,
        compiler_params=PARAMS,
        name="far_tiles",
    )(x, *operands)


def sum_other_kernel(dq, back_a, back_b, out, *, scale):
    rows = dq.shape[0]
    total = dq[...] * scale + back_a[rows:].astype(jnp.float32) + back_b[rows:].astype(jnp.float32)
    out[...] = total.astype(jnp.bfloat16)


def sum_other(dq, back_a, back_b, scale):
    return pl.pallas_call(
        functools.partial(sum_other_kernel, scale=scale),
        in_specs=[WHOLE] * 3,
        out_specs=WHOLE,
        out_shape=jax.ShapeDtypeStruct(dq.shape, jnp.bfloat16),
        compiler_params=PARAMS,
        name="sum_other",
    )(dq, back_a, back_b)


def finish_kernel(x_ref, dq_own, back_a, back_b, dkv_own, dkv_other, dq, dk, dv, buffer, sems, *, scale):
    rows, half = buffer.shape
    at_own = pl.ds(pl.multiple_of(x_ref[0] * half, LANES), half)
    at_other = pl.ds(pl.multiple_of((1 - x_ref[0]) * half, LANES), half)
    moves = (
        (dkv_own.at[0:rows], dk.at[:, at_own]),
        (dkv_own.at[rows : 2 * rows], dv.at[:, at_own]),
        (dkv_other.at[0:rows], dk.at[:, at_other]),
        (dkv_other.at[rows : 2 * rows], dv.at[:, at_other]),
    )
    copies = [pltpu.make_async_copy(a, b, sems.at[n]) for n, (a, b) in enumerate(moves)]
    for copy in copies:
        copy.start()
    total = (
        dq_own[...] * scale + back_a[0:rows].astype(jnp.float32) + back_b[0:rows].astype(jnp.float32)
    )
    buffer[...] = total.astype(jnp.bfloat16)
    copies.append(pltpu.make_async_copy(buffer, dq.at[:, at_own], sems.at[4]))
    copies[-1].start()
    for copy in copies:
        copy.wait()


def finish(x, dq_own, back_a, back_b, dkv_own, dkv_other, scale):
    rows, half = dq_own.shape
    return pl.pallas_call(
        functools.partial(finish_kernel, scale=scale),
        in_specs=[pl.BlockSpec(memory_space=pltpu.SMEM)] + [WHOLE] * 5,
        out_specs=[IN_HBM] * 3,
        out_shape=[jax.ShapeDtypeStruct((rows, 2 * half), jnp.bfloat16)] * 3,
        scratch_shapes=[pltpu.VMEM((rows, half), jnp.bfloat16), pltpu.SemaphoreType.DMA((5,))],
        compiler_params=PARAMS,
        name="finish",
    )(x, dq_own, back_a, back_b, dkv_own, dkv_other)


def place_kernel(x_ref, part, _, whole, sem):
    half = part.shape[1]
    at_other = pl.ds(pl.multiple_of((1 - x_ref[0]) * half, LANES), half)
    copy = pltpu.make_async_copy(part, whole.at[:, at_other], sem)
    copy.start()
    copy.wait()


def place(x, part, whole):
    return pl.pallas_call(
        place_kernel,
        in_specs=[pl.BlockSpec(memory_space=pltpu.SMEM), WHOLE, IN_HBM],
        out_specs=IN_HBM,
        out_shape=jax.ShapeDtypeStruct(whole.shape, whole.dtype),
        scratch_shapes=[pltpu.SemaphoreType.DMA],
        input_output_aliases={2: 0},
        compiler_params=PARAMS,
        name="place",
    )(x, part, whole)


def per_device(query_rows, key_rows, value_rows, layer_output, output_grad, log_norms):
    count = lax.axis_size("outer") * lax.axis_size("inner")
    index = lax.axis_index("outer") * lax.axis_size("inner") + lax.axis_index("inner")
    column, row = index % 2, index // 2 % 2
    x = jnp.stack([column, column ^ row]).astype(jnp.int32)
    head_size = query_rows.shape[1] // log_norms.shape[0]
    scale = head_size ** (-0.5)

    swap = [(i, i ^ 1) for i in range(count)]
    step_1 = [(i, i ^ 2) for i in range(count)]
    step_2 = [(i, ((i + 2) ^ 2) - 2) for i in range(count)]
    step_2 = [(i, j) for i, j in step_2 if 0 <= j < count]

    def send(a, perm):
        return lax.ppermute(a, AXES, perm)

    own, kv_own, to_other, kv_to_other = pack(
        x, query_rows, key_rows, value_rows, layer_output, output_grad, log_norms
    )
    other = send(to_other, swap)
    near_1, near_2 = send(own, step_1), send(own, step_2)
    kv_to_other, other = lax.optimization_barrier((kv_to_other, other))
    kv_other = send(kv_to_other, swap)
    far_1, far_2 = send(other, step_1), send(other, step_2)
    dq_own, dq_other, dq_1, dq_2, dkv = near_tiles(kv_own, own, other, near_1, near_2, scale)
    dq_own, dq_other, to_1, to_2, dkv_own, dkv_to_other = far_tiles(
        x, kv_own, kv_other, own, other, near_1, near_2, far_1, far_2,
        dq_own, dq_other, dq_1, dq_2, dkv, scale=scale,
    )
    dkv_other = send(dkv_to_other, swap)
    back_1, back_2 = send(to_1, step_1), send(to_2, step_2)
    dq_from_other = send(sum_other(dq_other, back_1, back_2, scale), swap)
    dq, dk, dv = finish(x, dq_own, back_1, back_2, dkv_own, dkv_other, scale)
    return place(x, dq_from_other, dq), dk, dv


def solution(mesh):
    rows = P(AXES, None)
    return jax.shard_map(
        per_device,
        mesh=mesh,
        in_specs=(rows, rows, rows, rows, rows, P(None, AXES)),
        out_specs=(rows, rows, rows),
        check_vma=False,
    )
```

```python
import functools

import jax
import jax.numpy as jnp
from jax import lax
from jax.experimental import pallas as pl
from jax.experimental.pallas import tpu as pltpu
from jax.sharding import PartitionSpec as P

AXES = ("outer", "inner")
LANES = 128
LOG2E = 1.4426950408889634
PAD = 16
WHOLE = pl.BlockSpec(memory_space=pltpu.VMEM)
IN_HBM = pl.BlockSpec(memory_space=pltpu.HBM)
PARAMS = pltpu.CompilerParams(vmem_limit_bytes=16 * 1024 * 1024)


def dot_nt(a, b):
    return lax.dot_general(a, b, (((1,), (1,)), ((), ())), preferred_element_type=jnp.float32)


def dot_nn(a, b):
    return lax.dot_general(a, b, (((1,), (0,)), ((), ())), preferred_element_type=jnp.float32)


def head_masks(dtype):
    lane = lax.broadcasted_iota(jnp.int32, (1, LANES), 1)
    first = jnp.where(lane < LANES // 2, 1.0, 0.0)
    return first.astype(dtype), (1.0 - first).astype(dtype)


def pack_kernel(x_ref, q, k, v, o, g, norms, msg, kv, msg_other, kv_other, outs, norm_buf, sems, norm_sem):
    rows, width = q.shape
    half = width // 2
    sides = ((1 - x_ref[0], msg_other, kv_other), (x_ref[0], msg, kv))
    norm_copy = pltpu.make_async_copy(norms, norm_buf, norm_sem)
    norm_copy.start()
    copies = []
    for at, (side, to, _) in enumerate(sides):
        columns = pl.ds(pl.multiple_of(side * half, LANES), half)
        moves = ((g, to.at[rows : 2 * rows]), (o, outs.at[at]), (q, to.at[0:rows]))
        copies.append([pltpu.make_async_copy(a.at[:, columns], b, sems.at[at, n]) for n, (a, b) in enumerate(moves)])
    later = []
    for at, (side, _, to) in enumerate(sides):
        columns = pl.ds(pl.multiple_of(side * half, LANES), half)
        moves = ((k, to.at[0:rows]), (v, to.at[rows : 2 * rows]))
        later += [pltpu.make_async_copy(a.at[:, columns], b, sems.at[at, 3 + n]) for n, (a, b) in enumerate(moves)]
    for copy in copies[0] + copies[1] + later:
        copy.start()
    norm_copy.wait()
    kv_other[2 * rows :] = jnp.zeros((PAD, half), kv_other.dtype)
    row = lax.broadcasted_iota(jnp.int32, (8, LANES), 0)
    lane = lax.broadcasted_iota(jnp.int32, (8, LANES), 1)
    pick = jnp.where(row == lane // (LANES // 2), 1.0, 0.0).astype(jnp.bfloat16)
    for at, (side, to, _) in enumerate(sides):
        copies[at][0].wait()
        copies[at][1].wait()
        for pair in range(half // LANES):
            span = slice(pair * LANES, (pair + 1) * LANES)
            product = outs[at, :, span].astype(jnp.float32) * to[rows : 2 * rows, span].astype(jnp.float32)
            high = product.astype(jnp.bfloat16)
            low = (product - high.astype(jnp.float32)).astype(jnp.bfloat16)
            delta = dot_nt(pick, high) + dot_nt(pick, low)
            first = 2 * (side * (half // LANES) + pair)
            terms = jnp.concatenate(
                [norm_buf[pl.ds(first, 1), :], norm_buf[pl.ds(first + 1, 1), :], delta[0:2]], axis=0
            )
            terms_high = terms.astype(jnp.bfloat16).astype(jnp.float32)
            both = jnp.concatenate([terms_high, terms - terms_high], axis=0)
            to[2 * rows : 2 * rows + 16, span] = jnp.concatenate(
                [both[:, :LANES], both[:, LANES:]], axis=0
            ).astype(jnp.bfloat16)
        copies[at][2].wait()
    for copy in later:
        copy.wait()


def pack(x, q, k, v, o, g, norms):
    rows, width = q.shape
    msg = jax.ShapeDtypeStruct((2 * rows + 16, width // 2), jnp.bfloat16)
    kv = jax.ShapeDtypeStruct((2 * rows, width // 2), jnp.bfloat16)
    kv_sent = jax.ShapeDtypeStruct((2 * rows + PAD, width // 2), jnp.bfloat16)
    return pl.pallas_call(
        pack_kernel,
        in_specs=[pl.BlockSpec(memory_space=pltpu.SMEM)] + [IN_HBM] * 6,
        out_specs=[WHOLE] * 4,
        out_shape=[msg, kv, msg, kv_sent],
        scratch_shapes=[
            pltpu.VMEM((2, rows, width // 2), jnp.bfloat16),
            pltpu.VMEM(norms.shape, jnp.float32),
            pltpu.SemaphoreType.DMA((2, 5)),
            pltpu.SemaphoreType.DMA,
        ],
        compiler_params=PARAMS,
        name="pack",
    )(x, *(pltpu.with_memory_space_constraint(a, pltpu.HBM) for a in (q, k, v, o, g, norms)))


def run_tiles(kv_refs, msg_refs, pairs, dq_in, dkv_in, dq_out, dkv_out, scale):
    rows, width = next(iter(dq_out.values())).shape
    half = LANES // 2
    masks = head_masks(jnp.bfloat16)
    key_side, query_side = {}, {}

    def span(group):
        return slice(group * LANES, (group + 1) * LANES)

    def keys_of(u, group):
        if (u, group) not in key_side:
            k, v = kv_refs[u][0:rows, span(group)], kv_refs[u][rows : 2 * rows, span(group)]
            kt = k.T
            sums = [None, None]
            if u in dkv_in:
                sums = [dkv_in[u][0:rows, span(group)], dkv_in[u][rows : 2 * rows, span(group)]]
            key_side[u, group] = (k, v, [kt[0:half], kt[half:LANES]], sums)
        return key_side[u, group]

    def queries_of(t, group):
        if (t, group) not in query_side:
            msg = msg_refs[t]
            q, g = msg[0:rows, span(group)], msg[rows : 2 * rows, span(group)]
            info = msg[2 * rows : 2 * rows + 16, span(group)].astype(jnp.float32)
            both = jnp.concatenate([info[0:8], info[8:16]], axis=1)
            terms = both[0:4] + both[4:8]
            query_side[t, group] = (
                [q * m for m in masks],
                [g * m for m in masks],
                terms[0:2] * LOG2E,
                terms[2:4],
                [None, None],
            )
        return query_side[t, group]

    def plus(a, b):
        return b if a is None else a + b

    items = [(group, u, t, h) for group in range(width // LANES) for u, t in pairs for h in range(2)]
    last_of = {}
    for group, u, t, h in items:
        last_of["key", u, group] = last_of["query", t, group] = (group, u, t, h)

    def products(item):
        group, u, t, h = item
        k, v, _, _ = keys_of(u, group)
        qs, gs = queries_of(t, group)[:2]
        return dot_nt(k, qs[h]), dot_nt(v, gs[h])

    def weigh(item, scores, grad_prob):
        group, u, t, h = item
        _, _, norms, deltas, _ = queries_of(t, group)
        probs = jnp.exp2(scores * (scale * LOG2E) - norms[h : h + 1])
        grad_score = probs * (grad_prob - deltas[h : h + 1])
        return probs.astype(jnp.bfloat16), grad_score.astype(jnp.bfloat16)

    def add_up(item, weights, grad_score):
        group, u, t, h = item
        _, _, kt, sums = keys_of(u, group)
        qs, gs, _, _, dq = queries_of(t, group)
        sums[1] = plus(sums[1], dot_nn(weights, gs[h]))
        sums[0] = plus(sums[0], dot_nn(grad_score, qs[h]))
        dq[h] = plus(dq[h], dot_nn(kt[h], grad_score))
        if last_of["query", t, group] == item:
            total = jnp.concatenate(dq, axis=0).T
            if t in dq_in:
                total = total + dq_in[t][:, span(group)]
            ref = dq_out[t]
            final = ref.dtype == jnp.bfloat16
            ref[:, span(group)] = (total * scale if final else total).astype(ref.dtype)
        if last_of["key", u, group] == item:
            ref = dkv_out[u]
            final = ref.dtype == jnp.bfloat16
            ref[0:rows, span(group)] = (sums[0] * scale if final else sums[0]).astype(ref.dtype)
            ref[rows : 2 * rows, span(group)] = sums[1].astype(ref.dtype)

    made, weighed = {}, {}
    for step in range(len(items) + 2):
        if step < len(items):
            made[step] = products(items[step])
        if 0 <= step - 1 < len(items):
            weighed[step - 1] = weigh(items[step - 1], *made.pop(step - 1))
        if 0 <= step - 2:
            add_up(items[step - 2], *weighed.pop(step - 2))


def near_kernel(kv, own, other, near_1, near_2, dq_own, dq_other, dq_1, dq_2, dkv, *, scale):
    run_tiles(
        {"own": kv},
        {"own": own, "other": other, "1": near_1, "2": near_2},
        [("own", t) for t in ("own", "1", "2", "other")],
        {},
        {},
        {"own": dq_own, "other": dq_other, "1": dq_1, "2": dq_2},
        {"own": dkv},
        scale,
    )


def near_tiles(kv, own, other, near_1, near_2, scale):
    rows, width = kv.shape[0] // 2, kv.shape[1]
    part = jax.ShapeDtypeStruct((rows, width), jnp.float32)
    return pl.pallas_call(
        functools.partial(near_kernel, scale=scale),
        in_specs=[WHOLE] * 5,
        out_specs=[WHOLE] * 5,
        out_shape=[part] * 4 + [jax.ShapeDtypeStruct(kv.shape, jnp.float32)],
        compiler_params=PARAMS,
        name="near_tiles",
    )(kv, own, other, near_1, near_2)


def mid_kernel(
    sides_ref, kv_other, own, other, near_1, near_2, dq_own, dq_other, dq_1, dq_2,
    out_own, out_other, back_near_a, back_near_b, dkv_other, near_b, dq_b, *, scale
):
    def sort(a, b):
        near_b[...] = b[0][...]
        dq_b[...] = b[1][...]
        back_near_a[...] = (a[1][...] * scale).astype(back_near_a.dtype)

    pl.when(sides_ref[0] == 1)(lambda: sort((near_1, dq_1), (near_2, dq_2)))
    pl.when(sides_ref[0] != 1)(lambda: sort((near_2, dq_2), (near_1, dq_1)))
    run_tiles(
        {"other": kv_other},
        {"own": own, "other": other, "near_b": near_b},
        [("other", t) for t in ("own", "other", "near_b")],
        {"own": dq_own, "other": dq_other, "near_b": dq_b},
        {},
        {"own": out_own, "other": out_other, "near_b": back_near_b},
        {"other": dkv_other},
        scale,
    )


def mid_tiles(sides, *operands, scale):
    msg, part_dq = operands[1], operands[5]
    rows, width = part_dq.shape
    part = jax.ShapeDtypeStruct((rows, width), jnp.float32)
    done = jax.ShapeDtypeStruct((rows, width), jnp.bfloat16)
    return pl.pallas_call(
        functools.partial(mid_kernel, scale=scale),
        in_specs=[pl.BlockSpec(memory_space=pltpu.SMEM)] + [WHOLE] * len(operands),
        out_specs=[WHOLE] * 5,
        out_shape=[part, part, done, done, jax.ShapeDtypeStruct((2 * rows, width), jnp.float32)],
        scratch_shapes=[pltpu.VMEM(msg.shape, msg.dtype), pltpu.VMEM(part.shape, part.dtype)],
        compiler_params=PARAMS,
        name="mid_tiles",
    )(sides, *operands)


def far_kernel(
    sides_ref, kv, kv_other, far_1, far_2, back_near_a, back_near_b, dkv, dkv_part,
    back_1, back_2, dkv_own, dkv_other, far_a, far_b, back_a, back_b, *, scale
):
    rows = back_near_a.shape[0]

    def sort(a, b):
        far_a[...] = a[...]
        far_b[...] = b[...]

    pl.when(sides_ref[0] == 1)(lambda: sort(far_1, far_2))
    pl.when(sides_ref[0] != 1)(lambda: sort(far_2, far_1))
    run_tiles(
        {"own": kv, "other": kv_other},
        {"far_a": far_a, "far_b": far_b},
        [("other", "far_b"), ("other", "far_a"), ("own", "far_a")],
        {},
        {"own": dkv, "other": dkv_part},
        {"far_a": back_a, "far_b": back_b},
        {"own": dkv_own, "other": dkv_other},
        scale,
    )

    dkv_other[2 * rows :] = jnp.zeros((PAD, dkv_other.shape[1]), dkv_other.dtype)

    def unsort(out_a, out_b):
        out_a[0:rows] = back_near_a[...]
        out_b[0:rows] = back_near_b[...]
        out_a[rows : 2 * rows] = back_a[...]
        out_b[rows : 2 * rows] = back_b[...]

    pl.when(sides_ref[0] == 1)(lambda: unsort(back_1, back_2))
    pl.when(sides_ref[0] != 1)(lambda: unsort(back_2, back_1))


def far_tiles(sides, *operands, scale):
    kv, msg, part = operands[0], operands[2], operands[4]
    done = jax.ShapeDtypeStruct(kv.shape, jnp.bfloat16)
    return pl.pallas_call(
        functools.partial(far_kernel, scale=scale),
        in_specs=[pl.BlockSpec(memory_space=pltpu.SMEM)] + [WHOLE] * len(operands),
        out_specs=[WHOLE] * 4,
        out_shape=[done] * 3 + [jax.ShapeDtypeStruct((kv.shape[0] + PAD, kv.shape[1]), jnp.bfloat16)],
        scratch_shapes=[pltpu.VMEM(msg.shape, msg.dtype)] * 2
        + [pltpu.VMEM(part.shape, part.dtype)] * 2,
        compiler_params=PARAMS,
        name="far_tiles",
    )(sides, *operands)


def sum_other_kernel(dq, back_a, back_b, out, *, scale):
    rows = dq.shape[0]
    total = dq[...] * scale + back_a[rows:].astype(jnp.float32) + back_b[rows:].astype(jnp.float32)
    out[...] = total.astype(jnp.bfloat16)


def sum_other(dq, back_a, back_b, scale):
    return pl.pallas_call(
        functools.partial(sum_other_kernel, scale=scale),
        in_specs=[WHOLE] * 3,
        out_specs=WHOLE,
        out_shape=jax.ShapeDtypeStruct(dq.shape, jnp.bfloat16),
        compiler_params=PARAMS,
        name="sum_other",
    )(dq, back_a, back_b)


def finish_kernel(x_ref, dq_own, back_a, back_b, dkv_own, dkv_other, dq, dk, dv, buffer, sems, *, scale):
    rows, half = buffer.shape
    at_own = pl.ds(pl.multiple_of(x_ref[0] * half, LANES), half)
    at_other = pl.ds(pl.multiple_of((1 - x_ref[0]) * half, LANES), half)
    moves = (
        (dkv_own.at[0:rows], dk.at[:, at_own]),
        (dkv_own.at[rows : 2 * rows], dv.at[:, at_own]),
        (dkv_other.at[0:rows], dk.at[:, at_other]),
        (dkv_other.at[rows : 2 * rows], dv.at[:, at_other]),
    )
    copies = [pltpu.make_async_copy(a, b, sems.at[n]) for n, (a, b) in enumerate(moves)]
    for copy in copies:
        copy.start()
    total = (
        dq_own[...] * scale + back_a[0:rows].astype(jnp.float32) + back_b[0:rows].astype(jnp.float32)
    )
    buffer[...] = total.astype(jnp.bfloat16)
    copies.append(pltpu.make_async_copy(buffer, dq.at[:, at_own], sems.at[4]))
    copies[-1].start()
    for copy in copies:
        copy.wait()


def finish(x, dq_own, back_a, back_b, dkv_own, dkv_other, scale):
    rows, half = dq_own.shape
    return pl.pallas_call(
        functools.partial(finish_kernel, scale=scale),
        in_specs=[pl.BlockSpec(memory_space=pltpu.SMEM)] + [WHOLE] * 5,
        out_specs=[IN_HBM] * 3,
        out_shape=[jax.ShapeDtypeStruct((rows, 2 * half), jnp.bfloat16)] * 3,
        scratch_shapes=[pltpu.VMEM((rows, half), jnp.bfloat16), pltpu.SemaphoreType.DMA((5,))],
        compiler_params=PARAMS,
        name="finish",
    )(x, dq_own, back_a, back_b, dkv_own, dkv_other)


def place_kernel(x_ref, part, _, whole, sem):
    half = part.shape[1]
    at_other = pl.ds(pl.multiple_of((1 - x_ref[0]) * half, LANES), half)
    copy = pltpu.make_async_copy(part, whole.at[:, at_other], sem)
    copy.start()
    copy.wait()


def place(x, part, whole):
    return pl.pallas_call(
        place_kernel,
        in_specs=[pl.BlockSpec(memory_space=pltpu.SMEM), WHOLE, IN_HBM],
        out_specs=IN_HBM,
        out_shape=jax.ShapeDtypeStruct(whole.shape, whole.dtype),
        scratch_shapes=[pltpu.SemaphoreType.DMA],
        input_output_aliases={2: 0},
        compiler_params=PARAMS,
        name="place",
    )(x, part, whole)


def per_device(query_rows, key_rows, value_rows, layer_output, output_grad, log_norms):
    count = lax.axis_size("outer") * lax.axis_size("inner")
    index = lax.axis_index("outer") * lax.axis_size("inner") + lax.axis_index("inner")
    column, row = index % 2, index // 2 % 2
    x = column.astype(jnp.int32).reshape(1)
    sides = (column ^ row).astype(jnp.int32).reshape(1)
    head_size = query_rows.shape[1] // log_norms.shape[0]
    scale = head_size ** (-0.5)

    swap = [(i, i ^ 1) for i in range(count)]
    step_1 = [(i, i ^ 2) for i in range(count)]
    step_2 = [(i, ((i + 2) ^ 2) - 2) for i in range(count)]
    step_2 = [(i, j) for i, j in step_2 if 0 <= j < count]

    def send(a, perm):
        return lax.ppermute(a, AXES, perm)

    own, kv_own, to_other, kv_to_other = pack(
        x, query_rows, key_rows, value_rows, layer_output, output_grad, log_norms
    )
    other = send(to_other, swap)
    near_1, near_2 = send(own, step_1), send(own, step_2)
    kv_to_other, other = lax.optimization_barrier((kv_to_other, other))
    kv_other = send(kv_to_other, swap)
    far_1, far_2 = send(other, step_1), send(other, step_2)
    dq_own, dq_other, dq_1, dq_2, dkv = near_tiles(kv_own, own, other, near_1, near_2, scale)
    dq_own, dq_other, back_near_a, back_near_b, dkv_part = mid_tiles(
        sides, kv_other, own, other, near_1, near_2, dq_own, dq_other, dq_1, dq_2, scale=scale
    )
    to_1, to_2, dkv_own, dkv_to_other = far_tiles(
        sides, kv_own, kv_other, far_1, far_2, back_near_a, back_near_b, dkv, dkv_part, scale=scale
    )
    dkv_other = send(dkv_to_other, swap)
    back_1, back_2 = send(to_1, step_1), send(to_2, step_2)
    dq_from_other = send(sum_other(dq_other, back_1, back_2, scale), swap)
    dq, dk, dv = finish(x, dq_own, back_1, back_2, dkv_own, dkv_other, scale)
    return place(x, dq_from_other, dq), dk, dv


def solution(mesh):
    rows = P(AXES, None)
    return jax.shard_map(
        per_device,
        mesh=mesh,
        in_specs=(rows, rows, rows, rows, rows, P(None, AXES)),
        out_specs=(rows, rows, rows),
        check_vma=False,
    )
```

```python
import functools

import jax
import jax.numpy as jnp
from jax import lax
from jax.experimental import pallas as pl
from jax.experimental.pallas import tpu as pltpu
from jax.sharding import PartitionSpec as P

AXES = ("outer", "inner")
LANES = 128
LOG2E = 1.4426950408889634
PAD = 16
WHOLE = pl.BlockSpec(memory_space=pltpu.VMEM)
IN_HBM = pl.BlockSpec(memory_space=pltpu.HBM)
PARAMS = pltpu.CompilerParams(vmem_limit_bytes=16 * 1024 * 1024)


def dot_nt(a, b):
    return lax.dot_general(a, b, (((1,), (1,)), ((), ())), preferred_element_type=jnp.float32)


def dot_nn(a, b):
    return lax.dot_general(a, b, (((1,), (0,)), ((), ())), preferred_element_type=jnp.float32)


def head_masks(dtype):
    lane = lax.broadcasted_iota(jnp.int32, (1, LANES), 1)
    first = jnp.where(lane < LANES // 2, 1.0, 0.0)
    return first.astype(dtype), (1.0 - first).astype(dtype)


def pack_kernel(x_ref, q, o, g, norms, *refs, other):
    if other:
        k, v, msg, kv, outs, norm_buf, sems = refs
    else:
        msg, outs, norm_buf, sems = refs
    rows, width = q.shape
    half = width // 2
    side = 1 - x_ref[0] if other else x_ref[0]
    columns = pl.ds(pl.multiple_of(side * half, LANES), half)
    moves = [(g.at[:, columns], msg.at[rows : 2 * rows]), (o.at[:, columns], outs), (norms, norm_buf)]
    moves.append((q.at[:, columns], msg.at[0:rows]))
    if other:
        moves += [(k.at[:, columns], kv.at[0:rows]), (v.at[:, columns], kv.at[rows : 2 * rows])]
    copies = [pltpu.make_async_copy(a, b, sems.at[n]) for n, (a, b) in enumerate(moves)]
    for copy in copies:
        copy.start()
    if other:
        kv[2 * rows :] = jnp.zeros((PAD, half), kv.dtype)
    row = lax.broadcasted_iota(jnp.int32, (8, LANES), 0)
    lane = lax.broadcasted_iota(jnp.int32, (8, LANES), 1)
    pick = jnp.where(row == lane // (LANES // 2), 1.0, 0.0).astype(jnp.bfloat16)
    for copy in copies[:3]:
        copy.wait()
    for pair in range(half // LANES):
        span = slice(pair * LANES, (pair + 1) * LANES)
        product = outs[:, span].astype(jnp.float32) * msg[rows : 2 * rows, span].astype(jnp.float32)
        high = product.astype(jnp.bfloat16)
        low = (product - high.astype(jnp.float32)).astype(jnp.bfloat16)
        delta = dot_nt(pick, high) + dot_nt(pick, low)
        first = 2 * (side * (half // LANES) + pair)
        terms = jnp.concatenate(
            [norm_buf[pl.ds(first, 1), :], norm_buf[pl.ds(first + 1, 1), :], delta[0:2]], axis=0
        )
        terms_high = terms.astype(jnp.bfloat16).astype(jnp.float32)
        both = jnp.concatenate([terms_high, terms - terms_high], axis=0)
        msg[2 * rows : 2 * rows + 16, span] = jnp.concatenate(
            [both[:, :LANES], both[:, LANES:]], axis=0
        ).astype(jnp.bfloat16)
    for copy in copies[3:]:
        copy.wait()


def pack(x, q, o, g, norms, *kv, name):
    rows, width = q.shape
    shapes = [jax.ShapeDtypeStruct((2 * rows + 16, width // 2), jnp.bfloat16)]
    if kv:
        shapes.append(jax.ShapeDtypeStruct((2 * rows + PAD, width // 2), jnp.bfloat16))
    operands = [pltpu.with_memory_space_constraint(a, pltpu.HBM) for a in (q, o, g, norms, *kv)]
    return pl.pallas_call(
        functools.partial(pack_kernel, other=bool(kv)),
        in_specs=[pl.BlockSpec(memory_space=pltpu.SMEM)] + [IN_HBM] * len(operands),
        out_specs=[WHOLE] * len(shapes),
        out_shape=shapes,
        scratch_shapes=[
            pltpu.VMEM((rows, width // 2), jnp.bfloat16),
            pltpu.VMEM(norms.shape, jnp.float32),
            pltpu.SemaphoreType.DMA((len(operands),)),
        ],
        compiler_params=PARAMS,
        name=name,
    )(x, *operands)


def load(source, rows, columns):
    if not isinstance(source, tuple):
        return source[rows, columns]
    flag, first, second = source
    return jnp.where(flag, first[rows, columns], second[rows, columns])


def run_tiles(kv_refs, msg_refs, pairs, dq_in, dkv_in, dq_out, dkv_out, scale):
    rows, width = next(iter(dq_out.values())).shape
    half = LANES // 2
    masks = head_masks(jnp.bfloat16)
    key_side, query_side = {}, {}

    def span(group):
        return slice(group * LANES, (group + 1) * LANES)

    def keys_of(u, group):
        if (u, group) not in key_side:
            k, v = kv_refs[u][0:rows, span(group)], kv_refs[u][rows : 2 * rows, span(group)]
            kt = k.T
            sums = [None, None]
            if u in dkv_in:
                sums = [dkv_in[u][0:rows, span(group)], dkv_in[u][rows : 2 * rows, span(group)]]
            key_side[u, group] = (k, v, [kt[0:half], kt[half:LANES]], sums)
        return key_side[u, group]

    def queries_of(t, group):
        if (t, group) not in query_side:
            q = load(msg_refs[t], slice(0, rows), span(group))
            g = load(msg_refs[t], slice(rows, 2 * rows), span(group))
            info = load(msg_refs[t], slice(2 * rows, 2 * rows + 16), span(group)).astype(jnp.float32)
            both = jnp.concatenate([info[0:8], info[8:16]], axis=1)
            terms = both[0:4] + both[4:8]
            query_side[t, group] = (
                [q * m for m in masks],
                [g * m for m in masks],
                terms[0:2] * LOG2E,
                terms[2:4],
                [None, None],
            )
        return query_side[t, group]

    def plus(a, b):
        return b if a is None else a + b

    items = [(group, u, t, h) for group in range(width // LANES) for u, t in pairs for h in range(2)]
    last_of = {}
    for group, u, t, h in items:
        last_of["key", u, group] = last_of["query", t, group] = (group, u, t, h)

    def products(item):
        group, u, t, h = item
        k, v, _, _ = keys_of(u, group)
        qs, gs = queries_of(t, group)[:2]
        return dot_nt(k, qs[h]), dot_nt(v, gs[h])

    def weigh(item, scores, grad_prob):
        group, u, t, h = item
        _, _, norms, deltas, _ = queries_of(t, group)
        probs = jnp.exp2(scores * (scale * LOG2E) - norms[h : h + 1])
        grad_score = probs * (grad_prob - deltas[h : h + 1])
        return probs.astype(jnp.bfloat16), grad_score.astype(jnp.bfloat16)

    def add_up(item, weights, grad_score):
        group, u, t, h = item
        _, _, kt, sums = keys_of(u, group)
        qs, gs, _, _, dq = queries_of(t, group)
        sums[1] = plus(sums[1], dot_nn(weights, gs[h]))
        sums[0] = plus(sums[0], dot_nn(grad_score, qs[h]))
        dq[h] = plus(dq[h], dot_nn(kt[h], grad_score))
        if last_of["query", t, group] == item:
            total = jnp.concatenate(dq, axis=0).T
            if t in dq_in:
                total = total + load(dq_in[t], slice(0, rows), span(group))
            ref = dq_out[t]
            final = ref.dtype == jnp.bfloat16
            ref[:, span(group)] = (total * scale if final else total).astype(ref.dtype)
        if last_of["key", u, group] == item:
            ref = dkv_out[u]
            final = ref.dtype == jnp.bfloat16
            ref[0:rows, span(group)] = (sums[0] * scale if final else sums[0]).astype(ref.dtype)
            ref[rows : 2 * rows, span(group)] = sums[1].astype(ref.dtype)

    made, weighed = {}, {}
    for step in range(len(items) + 2):
        if step < len(items):
            made[step] = products(items[step])
        if 0 <= step - 1 < len(items):
            weighed[step - 1] = weigh(items[step - 1], *made.pop(step - 1))
        if 0 <= step - 2:
            add_up(items[step - 2], *weighed.pop(step - 2))


def near_kernel(
    x_ref, k, v, own, other, near_1, near_2,
    dq_own, dq_other, dq_1, dq_2, dkv, kv, sems, *, scale
):
    rows, half = dq_own.shape
    columns = pl.ds(pl.multiple_of(x_ref[0] * half, LANES), half)
    moves = ((k, kv.at[0:rows]), (v, kv.at[rows : 2 * rows]))
    copies = [pltpu.make_async_copy(a.at[:, columns], b, sems.at[n]) for n, (a, b) in enumerate(moves)]
    for copy in copies:
        copy.start()
    for copy in copies:
        copy.wait()
    run_tiles(
        {"own": kv},
        {"own": own, "other": other, "1": near_1, "2": near_2},
        [("own", t) for t in ("own", "other", "1", "2")],
        {},
        {},
        {"own": dq_own, "other": dq_other, "1": dq_1, "2": dq_2},
        {"own": dkv},
        scale,
    )


def near_tiles(x, k, v, *msgs, scale):
    rows, width = k.shape[0], k.shape[1] // 2
    part = jax.ShapeDtypeStruct((rows, width), jnp.float32)
    sums = jax.ShapeDtypeStruct((2 * rows, width), jnp.float32)
    kv = jax.ShapeDtypeStruct((2 * rows, width), jnp.bfloat16)
    return pl.pallas_call(
        functools.partial(near_kernel, scale=scale),
        in_specs=[pl.BlockSpec(memory_space=pltpu.SMEM)] + [IN_HBM] * 2 + [WHOLE] * len(msgs),
        out_specs=[WHOLE] * 6,
        out_shape=[part] * 4 + [sums, kv],
        scratch_shapes=[pltpu.SemaphoreType.DMA((2,))],
        compiler_params=PARAMS,
        name="near_tiles",
    )(x, *(pltpu.with_memory_space_constraint(a, pltpu.HBM) for a in (k, v)), *msgs)


def mid_kernel(
    sides_ref, kv_other, own, other, near_1, near_2, dq_own, dq_other, dq_1, dq_2,
    out_own, out_other, back_near_a, back_near_b, dkv_other, *, scale
):
    first = sides_ref[0] == 1
    every = slice(None)
    back_near_a[...] = (load((first, dq_1, dq_2), every, every) * scale).astype(back_near_a.dtype)
    run_tiles(
        {"other": kv_other},
        {"own": own, "other": other, "near_b": (first, near_2, near_1)},
        [("other", t) for t in ("own", "other", "near_b")],
        {"own": dq_own, "other": dq_other, "near_b": (first, dq_2, dq_1)},
        {},
        {"own": out_own, "other": out_other, "near_b": back_near_b},
        {"other": dkv_other},
        scale,
    )


def mid_tiles(sides, *operands, scale):
    rows, width = operands[5].shape
    part = jax.ShapeDtypeStruct((rows, width), jnp.float32)
    done = jax.ShapeDtypeStruct((rows, width), jnp.bfloat16)
    return pl.pallas_call(
        functools.partial(mid_kernel, scale=scale),
        in_specs=[pl.BlockSpec(memory_space=pltpu.SMEM)] + [WHOLE] * len(operands),
        out_specs=[WHOLE] * 5,
        out_shape=[part, part, done, done, jax.ShapeDtypeStruct((2 * rows, width), jnp.float32)],
        compiler_params=PARAMS,
        name="mid_tiles",
    )(sides, *operands)


def far_kernel(
    sides_ref, relayed_ref, kv, kv_other, far_1, far_2, back_near_a, back_near_b, relayed, dkv_in, dkv_part_in,
    back_near_1, back_near_2, back_far_1, back_far_2, dkv_own, dkv_other, dkv, dkv_part, back_a, back_b, *, scale
):
    first = sides_ref[0] == 1
    every = slice(None)
    back_near_1[...] = load((first, back_near_a, back_near_b), every, every)
    back_near_2[...] = load((first, back_near_b, back_near_a), every, every)
    dkv_other[2 * back_a.shape[0] :] = jnp.zeros((PAD, dkv_other.shape[1]), dkv_other.dtype)

    def relayed_tiles(keys):
        run_tiles(
            {"own": kv, "other": kv_other},
            {"near": relayed},
            [(u, "near") for u in keys],
            {},
            {"own": dkv, "other": dkv_part},
            {"near": back_near_2},
            {"own": dkv, "other": dkv_part},
            scale,
        )

    here = relayed_ref[0] == 1
    pl.when(jnp.logical_and(here, first))(lambda: relayed_tiles(("own", "other")))
    pl.when(jnp.logical_and(here, jnp.logical_not(first)))(lambda: relayed_tiles(("own",)))
    run_tiles(
        {"own": kv, "other": kv_other},
        {"far_a": (first, far_1, far_2), "far_b": (first, far_2, far_1)},
        [("other", "far_b"), ("other", "far_a"), ("own", "far_a")],
        {},
        {"own": dkv, "other": dkv_part},
        {"far_a": back_a, "far_b": back_b},
        {"own": dkv_own, "other": dkv_other},
        scale,
    )
    back_far_1[...] = load((first, back_a, back_b), every, every)
    back_far_2[...] = load((first, back_b, back_a), every, every)


def far_tiles(sides, relayed_here, *operands, scale):
    kv, part, sums = operands[0], operands[4], operands[7]
    part_done = jax.ShapeDtypeStruct(part.shape, jnp.bfloat16)
    done = jax.ShapeDtypeStruct(kv.shape, jnp.bfloat16)
    sent = jax.ShapeDtypeStruct((kv.shape[0] + PAD, kv.shape[1]), jnp.bfloat16)
    results = pl.pallas_call(
        functools.partial(far_kernel, scale=scale),
        in_specs=[pl.BlockSpec(memory_space=pltpu.SMEM)] * 2 + [WHOLE] * len(operands),
        out_specs=[WHOLE] * 8,
        out_shape=[part_done] * 4 + [done, sent] + [jax.ShapeDtypeStruct(sums.shape, sums.dtype)] * 2,
        scratch_shapes=[pltpu.VMEM(part.shape, part.dtype)] * 2,
        input_output_aliases={9: 6, 10: 7},
        compiler_params=PARAMS,
        name="far_tiles",
    )(sides, relayed_here, *operands)
    return results[:6]


def sum_other_kernel(dq, back_a, back_b, out, *, scale):
    total = dq[...] * scale + back_a[...].astype(jnp.float32) + back_b[...].astype(jnp.float32)
    out[...] = total.astype(jnp.bfloat16)


def sum_other(dq, back_a, back_b, scale):
    return pl.pallas_call(
        functools.partial(sum_other_kernel, scale=scale),
        in_specs=[WHOLE] * 3,
        out_specs=WHOLE,
        out_shape=jax.ShapeDtypeStruct(dq.shape, jnp.bfloat16),
        compiler_params=PARAMS,
        name="sum_other",
    )(dq, back_a, back_b)


def finish_kernel(x_ref, dq_own, back_a, back_b, dkv_own, dkv_other, dq, dk, dv, buffer, sems, *, scale):
    rows, half = buffer.shape
    at_own = pl.ds(pl.multiple_of(x_ref[0] * half, LANES), half)
    at_other = pl.ds(pl.multiple_of((1 - x_ref[0]) * half, LANES), half)
    moves = (
        (dkv_own.at[0:rows], dk.at[:, at_own]),
        (dkv_own.at[rows : 2 * rows], dv.at[:, at_own]),
        (dkv_other.at[0:rows], dk.at[:, at_other]),
        (dkv_other.at[rows : 2 * rows], dv.at[:, at_other]),
    )
    copies = [pltpu.make_async_copy(a, b, sems.at[n]) for n, (a, b) in enumerate(moves)]
    for copy in copies:
        copy.start()
    total = (
        dq_own[...] * scale + back_a[...].astype(jnp.float32) + back_b[...].astype(jnp.float32)
    )
    buffer[...] = total.astype(jnp.bfloat16)
    copies.append(pltpu.make_async_copy(buffer, dq.at[:, at_own], sems.at[4]))
    copies[-1].start()
    for copy in copies:
        copy.wait()


def finish(x, dq_own, back_a, back_b, dkv_own, dkv_other, scale):
    rows, half = dq_own.shape
    return pl.pallas_call(
        functools.partial(finish_kernel, scale=scale),
        in_specs=[pl.BlockSpec(memory_space=pltpu.SMEM)] + [WHOLE] * 5,
        out_specs=[IN_HBM] * 3,
        out_shape=[jax.ShapeDtypeStruct((rows, 2 * half), jnp.bfloat16)] * 3,
        scratch_shapes=[pltpu.VMEM((rows, half), jnp.bfloat16), pltpu.SemaphoreType.DMA((5,))],
        compiler_params=PARAMS,
        name="finish",
    )(x, dq_own, back_a, back_b, dkv_own, dkv_other)


def place_kernel(x_ref, part, _, whole, sem):
    half = part.shape[1]
    at_other = pl.ds(pl.multiple_of((1 - x_ref[0]) * half, LANES), half)
    copy = pltpu.make_async_copy(part, whole.at[:, at_other], sem)
    copy.start()
    copy.wait()


def place(x, part, whole):
    return pl.pallas_call(
        place_kernel,
        in_specs=[pl.BlockSpec(memory_space=pltpu.SMEM), WHOLE, IN_HBM],
        out_specs=IN_HBM,
        out_shape=jax.ShapeDtypeStruct(whole.shape, whole.dtype),
        scratch_shapes=[pltpu.SemaphoreType.DMA],
        input_output_aliases={2: 0},
        compiler_params=PARAMS,
        name="place",
    )(x, part, whole)


def per_device(query_rows, key_rows, value_rows, layer_output, output_grad, log_norms):
    count = lax.axis_size("outer") * lax.axis_size("inner")
    index = lax.axis_index("outer") * lax.axis_size("inner") + lax.axis_index("inner")
    column, row = index % 2, index // 2 % 2
    x = column.astype(jnp.int32).reshape(1)
    sides = (column ^ row).astype(jnp.int32).reshape(1)
    head_size = query_rows.shape[1] // log_norms.shape[0]
    scale = head_size ** (-0.5)

    swap = [(i, i ^ 1) for i in range(count)]
    step_1 = [(i, i ^ 2) for i in range(count)]
    step_2 = [(i, ((i + 2) ^ 2) - 2) for i in range(count)]
    step_2 = [(i, j) for i, j in step_2 if 0 <= j < count]
    half = count // 2
    across = [(half - 2 + k, count - 2 + k) for k in range(2)] + [(half + k, k) for k in range(2)]
    onward = [(count - 2 + k, half + k) for k in range(2)] + [(k, half - 2 + k) for k in range(2)]
    step_2_own = [(i, j) for i, j in step_2 if (i < half) == (j < half)]
    relayed_here = ((index >= half - 2) & (index < half + 2)).astype(jnp.int32).reshape(1)

    def send(a, perm):
        return lax.ppermute(a, AXES, perm)

    to_other, kv_to_other = pack(
        x, query_rows, layer_output, output_grad, log_norms, key_rows, value_rows, name="pack_other"
    )
    (own,) = pack(x, query_rows, layer_output, output_grad, log_norms, name="pack_own")
    other = send(to_other, swap)
    near_1, near_2 = send(own, step_1), send(own, step_2_own)
    relayed = send(send(own, across), onward)
    kv_to_other, other = lax.optimization_barrier((kv_to_other, other))
    kv_other = send(kv_to_other, swap)
    far_1, far_2 = send(other, step_1), send(other, step_2)
    dq_own, dq_other, dq_1, dq_2, dkv, kv_own = near_tiles(
        x, key_rows, value_rows, own, other, near_1, near_2, scale=scale
    )
    dq_own, dq_other, back_near_a, back_near_b, dkv_part = mid_tiles(
        sides, kv_other, own, other, near_1, near_2,
        dq_own, dq_other, dq_1, dq_2, scale=scale,
    )
    near_to_1, near_to_2, far_to_1, far_to_2, dkv_own, dkv_to_other = far_tiles(
        sides, relayed_here, kv_own, kv_other, far_1, far_2, back_near_a, back_near_b, relayed,
        dkv, dkv_part, scale=scale,
    )
    dkv_other = send(dkv_to_other, swap)
    far_back_1, far_back_2 = send(far_to_1, step_1), send(far_to_2, step_2)
    back_1, back_2 = send(near_to_1, step_1), send(near_to_2, step_2)
    dq_from_other = send(sum_other(dq_other, far_back_1, far_back_2, scale), swap)
    dq, dk, dv = finish(x, dq_own, back_1, back_2, dkv_own, dkv_other, scale)
    return place(x, dq_from_other, dq), dk, dv


def solution(mesh):
    rows = P(AXES, None)
    return jax.shard_map(
        per_device,
        mesh=mesh,
        in_specs=(rows, rows, rows, rows, rows, P(None, AXES)),
        out_specs=(rows, rows, rows),
        check_vma=False,
    )
```

```python
import functools

import jax
import jax.numpy as jnp
from jax import lax
from jax.experimental import pallas as pl
from jax.experimental.pallas import tpu as pltpu
from jax.sharding import PartitionSpec as P

AXES = ("outer", "inner")
LANES = 128
LOG2E = 1.4426950408889634
PAD = 16
WHOLE = pl.BlockSpec(memory_space=pltpu.VMEM)
IN_HBM = pl.BlockSpec(memory_space=pltpu.HBM)
PARAMS = pltpu.CompilerParams(vmem_limit_bytes=16 * 1024 * 1024)


def dot_nt(a, b):
    return lax.dot_general(a, b, (((1,), (1,)), ((), ())), preferred_element_type=jnp.float32)


def dot_nn(a, b):
    return lax.dot_general(a, b, (((1,), (0,)), ((), ())), preferred_element_type=jnp.float32)


def head_masks(dtype):
    lane = lax.broadcasted_iota(jnp.int32, (1, LANES), 1)
    first = jnp.where(lane < LANES // 2, 1.0, 0.0)
    return first.astype(dtype), (1.0 - first).astype(dtype)


def pack_kernel(x_ref, q, o, g, norms, *refs, other):
    if other:
        msg, outs, norm_buf, sems = refs
    else:
        k, v, msg, kv, outs, norm_buf, sems = refs
    rows, width = q.shape
    half = width // 2
    side = 1 - x_ref[0] if other else x_ref[0]
    columns = pl.ds(pl.multiple_of(side * half, LANES), half)
    moves = [(g.at[:, columns], msg.at[rows : 2 * rows]), (o.at[:, columns], outs), (norms, norm_buf)]
    moves.append((q.at[:, columns], msg.at[0:rows]))
    if not other:
        away = pl.ds(pl.multiple_of((1 - side) * half, LANES), half)
        moves += [(k.at[:, away], kv.at[0:rows]), (v.at[:, away], kv.at[rows : 2 * rows])]
    copies = [pltpu.make_async_copy(a, b, sems.at[n]) for n, (a, b) in enumerate(moves)]
    for copy in copies:
        copy.start()
    if not other:
        kv[2 * rows :] = jnp.zeros((PAD, half), kv.dtype)
    row = lax.broadcasted_iota(jnp.int32, (8, LANES), 0)
    lane = lax.broadcasted_iota(jnp.int32, (8, LANES), 1)
    pick = jnp.where(row == lane // (LANES // 2), 1.0, 0.0).astype(jnp.bfloat16)
    for copy in copies[:3]:
        copy.wait()
    for pair in range(half // LANES):
        span = slice(pair * LANES, (pair + 1) * LANES)
        product = outs[:, span].astype(jnp.float32) * msg[rows : 2 * rows, span].astype(jnp.float32)
        high = product.astype(jnp.bfloat16)
        low = (product - high.astype(jnp.float32)).astype(jnp.bfloat16)
        delta = dot_nt(pick, high) + dot_nt(pick, low)
        first = 2 * (side * (half // LANES) + pair)
        terms = jnp.concatenate(
            [norm_buf[pl.ds(first, 1), :], norm_buf[pl.ds(first + 1, 1), :], delta[0:2]], axis=0
        )
        terms_high = terms.astype(jnp.bfloat16).astype(jnp.float32)
        both = jnp.concatenate([terms_high, terms - terms_high], axis=0)
        msg[2 * rows : 2 * rows + 16, span] = jnp.concatenate(
            [both[:, :LANES], both[:, LANES:]], axis=0
        ).astype(jnp.bfloat16)
    for copy in copies[3:]:
        copy.wait()


def pack(x, q, o, g, norms, *kv, name):
    rows, width = q.shape
    shapes = [jax.ShapeDtypeStruct((2 * rows + 16, width // 2), jnp.bfloat16)]
    if kv:
        shapes.append(jax.ShapeDtypeStruct((2 * rows + PAD, width // 2), jnp.bfloat16))
    operands = [pltpu.with_memory_space_constraint(a, pltpu.HBM) for a in (q, o, g, norms, *kv)]
    return pl.pallas_call(
        functools.partial(pack_kernel, other=not kv),
        in_specs=[pl.BlockSpec(memory_space=pltpu.SMEM)] + [IN_HBM] * len(operands),
        out_specs=[WHOLE] * len(shapes),
        out_shape=shapes,
        scratch_shapes=[
            pltpu.VMEM((rows, width // 2), jnp.bfloat16),
            pltpu.VMEM(norms.shape, jnp.float32),
            pltpu.SemaphoreType.DMA((len(operands),)),
        ],
        compiler_params=PARAMS,
        name=name,
    )(x, *operands)


def load(source, rows, columns):
    if not isinstance(source, tuple):
        return source[rows, columns]
    flag, first, second = source
    return jnp.where(flag, first[rows, columns], second[rows, columns])


def run_tiles(kv_refs, msg_refs, pairs, dq_in, dkv_in, dq_out, dkv_out, scale):
    rows, width = next(iter(dq_out.values())).shape
    half = LANES // 2
    masks = head_masks(jnp.bfloat16)
    key_side, query_side = {}, {}

    def span(group):
        return slice(group * LANES, (group + 1) * LANES)

    def keys_of(u, group):
        if (u, group) not in key_side:
            k, v = kv_refs[u][0:rows, span(group)], kv_refs[u][rows : 2 * rows, span(group)]
            kt = k.T
            sums = [None, None]
            if u in dkv_in:
                sums = [dkv_in[u][0:rows, span(group)], dkv_in[u][rows : 2 * rows, span(group)]]
            key_side[u, group] = (k, v, [kt[0:half], kt[half:LANES]], sums)
        return key_side[u, group]

    def queries_of(t, group):
        if (t, group) not in query_side:
            q = load(msg_refs[t], slice(0, rows), span(group))
            g = load(msg_refs[t], slice(rows, 2 * rows), span(group))
            info = load(msg_refs[t], slice(2 * rows, 2 * rows + 16), span(group)).astype(jnp.float32)
            both = jnp.concatenate([info[0:8], info[8:16]], axis=1)
            terms = both[0:4] + both[4:8]
            query_side[t, group] = (
                [q * m for m in masks],
                [g * m for m in masks],
                terms[0:2] * LOG2E,
                terms[2:4],
                [None, None],
            )
        return query_side[t, group]

    def plus(a, b):
        return b if a is None else a + b

    items = [(group, u, t, h) for group in range(width // LANES) for u, t in pairs for h in range(2)]
    last_of = {}
    for group, u, t, h in items:
        last_of["key", u, group] = last_of["query", t, group] = (group, u, t, h)

    def products(item):
        group, u, t, h = item
        k, v, _, _ = keys_of(u, group)
        qs, gs = queries_of(t, group)[:2]
        return dot_nt(k, qs[h]), dot_nt(v, gs[h])

    def weigh(item, scores, grad_prob):
        group, u, t, h = item
        _, _, norms, deltas, _ = queries_of(t, group)
        probs = jnp.exp2(scores * (scale * LOG2E) - norms[h : h + 1])
        grad_score = probs * (grad_prob - deltas[h : h + 1])
        return probs.astype(jnp.bfloat16), grad_score.astype(jnp.bfloat16)

    def add_up(item, weights, grad_score):
        group, u, t, h = item
        _, _, kt, sums = keys_of(u, group)
        qs, gs, _, _, dq = queries_of(t, group)
        sums[1] = plus(sums[1], dot_nn(weights, gs[h]))
        sums[0] = plus(sums[0], dot_nn(grad_score, qs[h]))
        dq[h] = plus(dq[h], dot_nn(kt[h], grad_score))
        if last_of["query", t, group] == item:
            total = jnp.concatenate(dq, axis=0).T
            if t in dq_in:
                total = total + load(dq_in[t], slice(0, rows), span(group))
            ref = dq_out[t]
            final = ref.dtype == jnp.bfloat16
            ref[:, span(group)] = (total * scale if final else total).astype(ref.dtype)
        if last_of["key", u, group] == item:
            ref = dkv_out[u]
            final = ref.dtype == jnp.bfloat16
            ref[0:rows, span(group)] = (sums[0] * scale if final else sums[0]).astype(ref.dtype)
            ref[rows : 2 * rows, span(group)] = sums[1].astype(ref.dtype)

    made, weighed = {}, {}
    for step in range(len(items) + 2):
        if step < len(items):
            made[step] = products(items[step])
        if 0 <= step - 1 < len(items):
            weighed[step - 1] = weigh(items[step - 1], *made.pop(step - 1))
        if 0 <= step - 2:
            add_up(items[step - 2], *weighed.pop(step - 2))


def near_kernel(
    x_ref, k, v, own, other, near_1, near_2,
    dq_own, dq_other, dq_1, dq_2, dkv, kv, sems, *, scale
):
    rows, half = dq_own.shape
    columns = pl.ds(pl.multiple_of(x_ref[0] * half, LANES), half)
    moves = ((k, kv.at[0:rows]), (v, kv.at[rows : 2 * rows]))
    copies = [pltpu.make_async_copy(a.at[:, columns], b, sems.at[n]) for n, (a, b) in enumerate(moves)]
    for copy in copies:
        copy.start()
    for copy in copies:
        copy.wait()
    run_tiles(
        {"own": kv},
        {"own": own, "other": other, "1": near_1, "2": near_2},
        [("own", t) for t in ("own", "other", "1", "2")],
        {},
        {},
        {"own": dq_own, "other": dq_other, "1": dq_1, "2": dq_2},
        {"own": dkv},
        scale,
    )


def near_tiles(x, k, v, *msgs, scale):
    rows, width = k.shape[0], k.shape[1] // 2
    part = jax.ShapeDtypeStruct((rows, width), jnp.float32)
    sums = jax.ShapeDtypeStruct((2 * rows, width), jnp.float32)
    kv = jax.ShapeDtypeStruct((2 * rows, width), jnp.bfloat16)
    return pl.pallas_call(
        functools.partial(near_kernel, scale=scale),
        in_specs=[pl.BlockSpec(memory_space=pltpu.SMEM)] + [IN_HBM] * 2 + [WHOLE] * len(msgs),
        out_specs=[WHOLE] * 6,
        out_shape=[part] * 4 + [sums, kv],
        scratch_shapes=[pltpu.SemaphoreType.DMA((2,))],
        compiler_params=PARAMS,
        name="near_tiles",
    )(x, *(pltpu.with_memory_space_constraint(a, pltpu.HBM) for a in (k, v)), *msgs)


def mid_kernel(
    sides_ref, kv_other, own, other, near_1, near_2, dq_own, dq_other, dq_1, dq_2,
    out_own, out_other, back_near_a, back_near_b, dkv_other, *, scale
):
    first = sides_ref[0] == 1
    every = slice(None)
    back_near_a[...] = (load((first, dq_1, dq_2), every, every) * scale).astype(back_near_a.dtype)
    run_tiles(
        {"other": kv_other},
        {"own": own, "other": other, "near_b": (first, near_2, near_1)},
        [("other", t) for t in ("own", "other", "near_b")],
        {"own": dq_own, "other": dq_other, "near_b": (first, dq_2, dq_1)},
        {},
        {"own": out_own, "other": out_other, "near_b": back_near_b},
        {"other": dkv_other},
        scale,
    )


def mid_tiles(sides, *operands, scale):
    rows, width = operands[5].shape
    part = jax.ShapeDtypeStruct((rows, width), jnp.float32)
    done = jax.ShapeDtypeStruct((rows, width), jnp.bfloat16)
    return pl.pallas_call(
        functools.partial(mid_kernel, scale=scale),
        in_specs=[pl.BlockSpec(memory_space=pltpu.SMEM)] + [WHOLE] * len(operands),
        out_specs=[WHOLE] * 5,
        out_shape=[part, part, done, done, jax.ShapeDtypeStruct((2 * rows, width), jnp.float32)],
        compiler_params=PARAMS,
        name="mid_tiles",
    )(sides, *operands)


def far_kernel(
    sides_ref, relayed_ref, kv, kv_other, far_1, far_2, back_near_a, back_near_b, relayed, dkv_in, dkv_part_in,
    back_near_1, back_near_2, back_far_1, back_far_2, dkv_own, dkv_other, dkv, dkv_part, back_a, back_b, *, scale
):
    first = sides_ref[0] == 1
    every = slice(None)
    back_near_1[...] = load((first, back_near_a, back_near_b), every, every)
    back_near_2[...] = load((first, back_near_b, back_near_a), every, every)
    dkv_other[2 * back_a.shape[0] :] = jnp.zeros((PAD, dkv_other.shape[1]), dkv_other.dtype)

    def relayed_tiles(keys):
        run_tiles(
            {"own": kv, "other": kv_other},
            {"near": relayed},
            [(u, "near") for u in keys],
            {},
            {"own": dkv, "other": dkv_part},
            {"near": back_near_2},
            {"own": dkv, "other": dkv_part},
            scale,
        )

    here = relayed_ref[0] == 1
    pl.when(jnp.logical_and(here, first))(lambda: relayed_tiles(("own", "other")))
    pl.when(jnp.logical_and(here, jnp.logical_not(first)))(lambda: relayed_tiles(("own",)))
    run_tiles(
        {"own": kv, "other": kv_other},
        {"far_a": (first, far_1, far_2), "far_b": (first, far_2, far_1)},
        [("other", "far_b"), ("other", "far_a"), ("own", "far_a")],
        {},
        {"own": dkv, "other": dkv_part},
        {"far_a": back_a, "far_b": back_b},
        {"own": dkv_own, "other": dkv_other},
        scale,
    )
    back_far_1[...] = load((first, back_a, back_b), every, every)
    back_far_2[...] = load((first, back_b, back_a), every, every)


def far_tiles(sides, relayed_here, *operands, scale):
    kv, part, sums = operands[0], operands[4], operands[7]
    part_done = jax.ShapeDtypeStruct(part.shape, jnp.bfloat16)
    done = jax.ShapeDtypeStruct(kv.shape, jnp.bfloat16)
    sent = jax.ShapeDtypeStruct((kv.shape[0] + PAD, kv.shape[1]), jnp.bfloat16)
    results = pl.pallas_call(
        functools.partial(far_kernel, scale=scale),
        in_specs=[pl.BlockSpec(memory_space=pltpu.SMEM)] * 2 + [WHOLE] * len(operands),
        out_specs=[WHOLE] * 8,
        out_shape=[part_done] * 4 + [done, sent] + [jax.ShapeDtypeStruct(sums.shape, sums.dtype)] * 2,
        scratch_shapes=[pltpu.VMEM(part.shape, part.dtype)] * 2,
        input_output_aliases={9: 6, 10: 7},
        compiler_params=PARAMS,
        name="far_tiles",
    )(sides, relayed_here, *operands)
    return results[:6]


def sum_other_kernel(dq, back_a, back_b, out, *, scale):
    total = dq[...] * scale + back_a[...].astype(jnp.float32) + back_b[...].astype(jnp.float32)
    out[...] = total.astype(jnp.bfloat16)


def sum_other(dq, back_a, back_b, scale):
    return pl.pallas_call(
        functools.partial(sum_other_kernel, scale=scale),
        in_specs=[WHOLE] * 3,
        out_specs=WHOLE,
        out_shape=jax.ShapeDtypeStruct(dq.shape, jnp.bfloat16),
        compiler_params=PARAMS,
        name="sum_other",
    )(dq, back_a, back_b)


def finish_kernel(x_ref, dq_own, back_a, back_b, dkv_own, dkv_other, dq, dk, dv, buffer, sems, *, scale):
    rows, half = buffer.shape
    at_own = pl.ds(pl.multiple_of(x_ref[0] * half, LANES), half)
    at_other = pl.ds(pl.multiple_of((1 - x_ref[0]) * half, LANES), half)
    moves = (
        (dkv_own.at[0:rows], dk.at[:, at_own]),
        (dkv_own.at[rows : 2 * rows], dv.at[:, at_own]),
        (dkv_other.at[0:rows], dk.at[:, at_other]),
        (dkv_other.at[rows : 2 * rows], dv.at[:, at_other]),
    )
    copies = [pltpu.make_async_copy(a, b, sems.at[n]) for n, (a, b) in enumerate(moves)]
    for copy in copies:
        copy.start()
    total = (
        dq_own[...] * scale + back_a[...].astype(jnp.float32) + back_b[...].astype(jnp.float32)
    )
    buffer[...] = total.astype(jnp.bfloat16)
    copies.append(pltpu.make_async_copy(buffer, dq.at[:, at_own], sems.at[4]))
    copies[-1].start()
    for copy in copies:
        copy.wait()


def finish(x, dq_own, back_a, back_b, dkv_own, dkv_other, scale):
    rows, half = dq_own.shape
    return pl.pallas_call(
        functools.partial(finish_kernel, scale=scale),
        in_specs=[pl.BlockSpec(memory_space=pltpu.SMEM)] + [WHOLE] * 5,
        out_specs=[IN_HBM] * 3,
        out_shape=[jax.ShapeDtypeStruct((rows, 2 * half), jnp.bfloat16)] * 3,
        scratch_shapes=[pltpu.VMEM((rows, half), jnp.bfloat16), pltpu.SemaphoreType.DMA((5,))],
        compiler_params=PARAMS,
        name="finish",
    )(x, dq_own, back_a, back_b, dkv_own, dkv_other)


def place_kernel(x_ref, part, _, whole, sem):
    half = part.shape[1]
    at_other = pl.ds(pl.multiple_of((1 - x_ref[0]) * half, LANES), half)
    copy = pltpu.make_async_copy(part, whole.at[:, at_other], sem)
    copy.start()
    copy.wait()


def place(x, part, whole):
    return pl.pallas_call(
        place_kernel,
        in_specs=[pl.BlockSpec(memory_space=pltpu.SMEM), WHOLE, IN_HBM],
        out_specs=IN_HBM,
        out_shape=jax.ShapeDtypeStruct(whole.shape, whole.dtype),
        scratch_shapes=[pltpu.SemaphoreType.DMA],
        input_output_aliases={2: 0},
        compiler_params=PARAMS,
        name="place",
    )(x, part, whole)


def per_device(query_rows, key_rows, value_rows, layer_output, output_grad, log_norms):
    count = lax.axis_size("outer") * lax.axis_size("inner")
    index = lax.axis_index("outer") * lax.axis_size("inner") + lax.axis_index("inner")
    column, row = index % 2, index // 2 % 2
    x = column.astype(jnp.int32).reshape(1)
    sides = (column ^ row).astype(jnp.int32).reshape(1)
    head_size = query_rows.shape[1] // log_norms.shape[0]
    scale = head_size ** (-0.5)

    swap = [(i, i ^ 1) for i in range(count)]
    step_1 = [(i, i ^ 2) for i in range(count)]
    step_2 = [(i, ((i + 2) ^ 2) - 2) for i in range(count)]
    step_2 = [(i, j) for i, j in step_2 if 0 <= j < count]
    half = count // 2
    across = [(half - 2 + k, count - 2 + k) for k in range(2)] + [(half + k, k) for k in range(2)]
    onward = [(count - 2 + k, half + k) for k in range(2)] + [(k, half - 2 + k) for k in range(2)]
    step_2_own = [(i, j) for i, j in step_2 if (i < half) == (j < half)]
    relayed_here = ((index >= half - 2) & (index < half + 2)).astype(jnp.int32).reshape(1)

    def send(a, perm):
        return lax.ppermute(a, AXES, perm)

    (to_other,) = pack(x, query_rows, layer_output, output_grad, log_norms, name="pack_other")
    own, kv_to_other = pack(
        x, query_rows, layer_output, output_grad, log_norms, key_rows, value_rows, name="pack_own"
    )
    other = send(to_other, swap)
    near_1, near_2 = send(own, step_1), send(own, step_2_own)
    relayed = send(send(own, across), onward)
    kv_to_other, other = lax.optimization_barrier((kv_to_other, other))
    kv_other = send(kv_to_other, swap)
    far_1, far_2 = send(other, step_1), send(other, step_2)
    dq_own, dq_other, dq_1, dq_2, dkv, kv_own = near_tiles(
        x, key_rows, value_rows, own, other, near_1, near_2, scale=scale
    )
    dq_own, dq_other, back_near_a, back_near_b, dkv_part = mid_tiles(
        sides, kv_other, own, other, near_1, near_2,
        dq_own, dq_other, dq_1, dq_2, scale=scale,
    )
    near_to_1, near_to_2, far_to_1, far_to_2, dkv_own, dkv_to_other = far_tiles(
        sides, relayed_here, kv_own, kv_other, far_1, far_2, back_near_a, back_near_b, relayed,
        dkv, dkv_part, scale=scale,
    )
    dkv_other = send(dkv_to_other, swap)
    far_back_1, far_back_2 = send(far_to_1, step_1), send(far_to_2, step_2)
    back_1, back_2 = send(near_to_1, step_1), send(near_to_2, step_2)
    dq_from_other = send(sum_other(dq_other, far_back_1, far_back_2, scale), swap)
    dq, dk, dv = finish(x, dq_own, back_1, back_2, dkv_own, dkv_other, scale)
    return place(x, dq_from_other, dq), dk, dv


def solution(mesh):
    rows = P(AXES, None)
    return jax.shard_map(
        per_device,
        mesh=mesh,
        in_specs=(rows, rows, rows, rows, rows, P(None, AXES)),
        out_specs=(rows, rows, rows),
        check_vma=False,
    )
```

```python
import functools

import jax
import jax.numpy as jnp
from jax import lax
from jax.experimental import pallas as pl
from jax.experimental.pallas import tpu as pltpu
from jax.sharding import PartitionSpec as P

AXES = ("outer", "inner")
LANES = 128
LOG2E = 1.4426950408889634
PAD = 16
WHOLE = pl.BlockSpec(memory_space=pltpu.VMEM)
IN_HBM = pl.BlockSpec(memory_space=pltpu.HBM)
PARAMS = pltpu.CompilerParams(vmem_limit_bytes=16 * 1024 * 1024)


def dot_nt(a, b):
    return lax.dot_general(a, b, (((1,), (1,)), ((), ())), preferred_element_type=jnp.float32)


def dot_nn(a, b):
    return lax.dot_general(a, b, (((1,), (0,)), ((), ())), preferred_element_type=jnp.float32)


def head_masks(dtype):
    lane = lax.broadcasted_iota(jnp.int32, (1, LANES), 1)
    first = jnp.where(lane < LANES // 2, 1.0, 0.0)
    return first.astype(dtype), (1.0 - first).astype(dtype)


def pack_kernel(x_ref, q, o, g, norms, *refs, other):
    if other:
        msg, outs, norm_buf, sems = refs
    else:
        k, v, msg, kv, outs, norm_buf, sems = refs
    rows, width = q.shape
    half = width // 2
    side = 1 - x_ref[0] if other else x_ref[0]
    columns = pl.ds(pl.multiple_of(side * half, LANES), half)
    moves = [(g.at[:, columns], msg.at[rows : 2 * rows]), (o.at[:, columns], outs), (norms, norm_buf)]
    moves.append((q.at[:, columns], msg.at[0:rows]))
    if not other:
        away = pl.ds(pl.multiple_of((1 - side) * half, LANES), half)
        moves += [(k.at[:, away], kv.at[0:rows]), (v.at[:, away], kv.at[rows : 2 * rows])]
    copies = [pltpu.make_async_copy(a, b, sems.at[n]) for n, (a, b) in enumerate(moves)]
    for copy in copies:
        copy.start()
    if not other:
        kv[2 * rows :] = jnp.zeros((PAD, half), kv.dtype)
    row = lax.broadcasted_iota(jnp.int32, (8, LANES), 0)
    lane = lax.broadcasted_iota(jnp.int32, (8, LANES), 1)
    pick = jnp.where(row == lane // (LANES // 2), 1.0, 0.0).astype(jnp.bfloat16)
    for copy in copies[:3]:
        copy.wait()
    for pair in range(half // LANES):
        span = slice(pair * LANES, (pair + 1) * LANES)
        product = outs[:, span].astype(jnp.float32) * msg[rows : 2 * rows, span].astype(jnp.float32)
        high = product.astype(jnp.bfloat16)
        low = (product - high.astype(jnp.float32)).astype(jnp.bfloat16)
        delta = dot_nt(pick, high) + dot_nt(pick, low)
        first = 2 * (side * (half // LANES) + pair)
        terms = jnp.concatenate(
            [norm_buf[pl.ds(first, 1), :], norm_buf[pl.ds(first + 1, 1), :], delta[0:2]], axis=0
        )
        terms_high = terms.astype(jnp.bfloat16).astype(jnp.float32)
        both = jnp.concatenate([terms_high, terms - terms_high], axis=0)
        msg[2 * rows : 2 * rows + 16, span] = jnp.concatenate(
            [both[:, :LANES], both[:, LANES:]], axis=0
        ).astype(jnp.bfloat16)
    for copy in copies[3:]:
        copy.wait()


def pack(x, q, o, g, norms, *kv, name):
    rows, width = q.shape
    shapes = [jax.ShapeDtypeStruct((2 * rows + 16, width // 2), jnp.bfloat16)]
    if kv:
        shapes.append(jax.ShapeDtypeStruct((2 * rows + PAD, width // 2), jnp.bfloat16))
    operands = [pltpu.with_memory_space_constraint(a, pltpu.HBM) for a in (q, o, g, norms, *kv)]
    return pl.pallas_call(
        functools.partial(pack_kernel, other=not kv),
        in_specs=[pl.BlockSpec(memory_space=pltpu.SMEM)] + [IN_HBM] * len(operands),
        out_specs=[WHOLE] * len(shapes),
        out_shape=shapes,
        scratch_shapes=[
            pltpu.VMEM((rows, width // 2), jnp.bfloat16),
            pltpu.VMEM(norms.shape, jnp.float32),
            pltpu.SemaphoreType.DMA((len(operands),)),
        ],
        compiler_params=PARAMS,
        name=name,
    )(x, *operands)


def load(source, rows, columns):
    if not isinstance(source, tuple):
        return source[rows, columns]
    flag, first, second = source
    return jnp.where(flag, first[rows, columns], second[rows, columns])


def run_tiles(kv_refs, msg_refs, pairs, dq_in, dkv_in, dq_out, dkv_out, scale, arrive=None):
    rows, width = next(iter(dq_out.values())).shape
    half = LANES // 2
    masks = head_masks(jnp.bfloat16)
    key_side, query_side = {}, {}

    def span(group):
        return slice(group * LANES, (group + 1) * LANES)

    def keys_of(u, group):
        if (u, group) not in key_side:
            if arrive is not None:
                arrive(group)
            k, v = kv_refs[u][0:rows, span(group)], kv_refs[u][rows : 2 * rows, span(group)]
            kt = k.T
            sums = [None, None]
            if u in dkv_in:
                sums = [dkv_in[u][0:rows, span(group)], dkv_in[u][rows : 2 * rows, span(group)]]
            key_side[u, group] = (k, v, [kt[0:half], kt[half:LANES]], sums)
        return key_side[u, group]

    def queries_of(t, group):
        if (t, group) not in query_side:
            q = load(msg_refs[t], slice(0, rows), span(group))
            g = load(msg_refs[t], slice(rows, 2 * rows), span(group))
            info = load(msg_refs[t], slice(2 * rows, 2 * rows + 16), span(group)).astype(jnp.float32)
            both = jnp.concatenate([info[0:8], info[8:16]], axis=1)
            terms = both[0:4] + both[4:8]
            query_side[t, group] = (
                [q * m for m in masks],
                [g * m for m in masks],
                terms[0:2] * LOG2E,
                terms[2:4],
                [None, None],
            )
        return query_side[t, group]

    def plus(a, b):
        return b if a is None else a + b

    items = [(group, u, t, h) for group in range(width // LANES) for u, t in pairs for h in range(2)]
    last_of = {}
    for group, u, t, h in items:
        last_of["key", u, group] = last_of["query", t, group] = (group, u, t, h)

    def products(item):
        group, u, t, h = item
        k, v, _, _ = keys_of(u, group)
        qs, gs = queries_of(t, group)[:2]
        return dot_nt(k, qs[h]), dot_nt(v, gs[h])

    def weigh(item, scores, grad_prob):
        group, u, t, h = item
        _, _, norms, deltas, _ = queries_of(t, group)
        probs = jnp.exp2(scores * (scale * LOG2E) - norms[h : h + 1])
        grad_score = probs * (grad_prob - deltas[h : h + 1])
        return probs.astype(jnp.bfloat16), grad_score.astype(jnp.bfloat16)

    def add_up(item, weights, grad_score):
        group, u, t, h = item
        _, _, kt, sums = keys_of(u, group)
        qs, gs, _, _, dq = queries_of(t, group)
        sums[1] = plus(sums[1], dot_nn(weights, gs[h]))
        sums[0] = plus(sums[0], dot_nn(grad_score, qs[h]))
        dq[h] = plus(dq[h], dot_nn(kt[h], grad_score))
        if last_of["query", t, group] == item:
            total = jnp.concatenate(dq, axis=0).T
            if t in dq_in:
                total = total + load(dq_in[t], slice(0, rows), span(group))
            ref = dq_out[t]
            final = ref.dtype == jnp.bfloat16
            ref[:, span(group)] = (total * scale if final else total).astype(ref.dtype)
        if last_of["key", u, group] == item:
            ref = dkv_out[u]
            final = ref.dtype == jnp.bfloat16
            ref[0:rows, span(group)] = (sums[0] * scale if final else sums[0]).astype(ref.dtype)
            ref[rows : 2 * rows, span(group)] = sums[1].astype(ref.dtype)

    made, weighed = {}, {}
    for step in range(len(items) + 2):
        if step < len(items):
            made[step] = products(items[step])
        if 0 <= step - 1 < len(items):
            weighed[step - 1] = weigh(items[step - 1], *made.pop(step - 1))
        if 0 <= step - 2:
            add_up(items[step - 2], *weighed.pop(step - 2))


def near_kernel(
    x_ref, k, v, own, other, near_1, near_2,
    dq_own, dq_other, dq_1, dq_2, dkv, kv, sems, *, scale
):
    rows, half = dq_own.shape
    copies = []
    for group in range(half // LANES):
        columns = pl.ds(pl.multiple_of(x_ref[0] * half + group * LANES, LANES), LANES)
        span = slice(group * LANES, (group + 1) * LANES)
        moves = ((k, kv.at[0:rows, span]), (v, kv.at[rows : 2 * rows, span]))
        copies.append([pltpu.make_async_copy(a.at[:, columns], b, sems.at[group, n]) for n, (a, b) in enumerate(moves)])
    for copy in sum(copies, []):
        copy.start()

    def arrive(group):
        for copy in copies[group]:
            copy.wait()

    run_tiles(
        {"own": kv},
        {"own": own, "other": other, "1": near_1, "2": near_2},
        [("own", t) for t in ("own", "other", "1", "2")],
        {},
        {},
        {"own": dq_own, "other": dq_other, "1": dq_1, "2": dq_2},
        {"own": dkv},
        scale,
        arrive,
    )


def near_tiles(x, k, v, *msgs, scale):
    rows, width = k.shape[0], k.shape[1] // 2
    part = jax.ShapeDtypeStruct((rows, width), jnp.float32)
    sums = jax.ShapeDtypeStruct((2 * rows, width), jnp.float32)
    kv = jax.ShapeDtypeStruct((2 * rows, width), jnp.bfloat16)
    return pl.pallas_call(
        functools.partial(near_kernel, scale=scale),
        in_specs=[pl.BlockSpec(memory_space=pltpu.SMEM)] + [IN_HBM] * 2 + [WHOLE] * len(msgs),
        out_specs=[WHOLE] * 6,
        out_shape=[part] * 4 + [sums, kv],
        scratch_shapes=[pltpu.SemaphoreType.DMA((width // LANES, 2))],
        compiler_params=PARAMS,
        name="near_tiles",
    )(x, *(pltpu.with_memory_space_constraint(a, pltpu.HBM) for a in (k, v)), *msgs)


def mid_kernel(
    sides_ref, kv_other, own, other, near_1, near_2, dq_own, dq_other, dq_1, dq_2,
    out_own, out_other, back_near_a, back_near_b, dkv_other, *, scale
):
    first = sides_ref[0] == 1
    every = slice(None)
    back_near_a[...] = (load((first, dq_1, dq_2), every, every) * scale).astype(back_near_a.dtype)
    run_tiles(
        {"other": kv_other},
        {"own": own, "other": other, "near_b": (first, near_2, near_1)},
        [("other", t) for t in ("own", "other", "near_b")],
        {"own": dq_own, "other": dq_other, "near_b": (first, dq_2, dq_1)},
        {},
        {"own": out_own, "other": out_other, "near_b": back_near_b},
        {"other": dkv_other},
        scale,
    )


def mid_tiles(sides, *operands, scale):
    rows, width = operands[5].shape
    part = jax.ShapeDtypeStruct((rows, width), jnp.float32)
    done = jax.ShapeDtypeStruct((rows, width), jnp.bfloat16)
    return pl.pallas_call(
        functools.partial(mid_kernel, scale=scale),
        in_specs=[pl.BlockSpec(memory_space=pltpu.SMEM)] + [WHOLE] * len(operands),
        out_specs=[WHOLE] * 5,
        out_shape=[part, part, done, done, jax.ShapeDtypeStruct((2 * rows, width), jnp.float32)],
        compiler_params=PARAMS,
        name="mid_tiles",
    )(sides, *operands)


def far_kernel(
    sides_ref, relayed_ref, kv, kv_other, far_1, far_2, back_near_a, back_near_b, relayed, dkv_in, dkv_part_in,
    back_near_1, back_near_2, back_far_1, back_far_2, dkv_own, dkv_other, dkv, dkv_part, back_a, back_b, *, scale
):
    first = sides_ref[0] == 1
    every = slice(None)
    back_near_1[...] = load((first, back_near_a, back_near_b), every, every)
    back_near_2[...] = load((first, back_near_b, back_near_a), every, every)
    dkv_other[2 * back_a.shape[0] :] = jnp.zeros((PAD, dkv_other.shape[1]), dkv_other.dtype)

    def relayed_tiles(keys):
        run_tiles(
            {"own": kv, "other": kv_other},
            {"near": relayed},
            [(u, "near") for u in keys],
            {},
            {"own": dkv, "other": dkv_part},
            {"near": back_near_2},
            {"own": dkv, "other": dkv_part},
            scale,
        )

    here = relayed_ref[0] == 1
    pl.when(jnp.logical_and(here, first))(lambda: relayed_tiles(("own", "other")))
    pl.when(jnp.logical_and(here, jnp.logical_not(first)))(lambda: relayed_tiles(("own",)))
    run_tiles(
        {"own": kv, "other": kv_other},
        {"far_a": (first, far_1, far_2), "far_b": (first, far_2, far_1)},
        [("other", "far_b"), ("other", "far_a"), ("own", "far_a")],
        {},
        {"own": dkv, "other": dkv_part},
        {"far_a": back_a, "far_b": back_b},
        {"own": dkv_own, "other": dkv_other},
        scale,
    )
    back_far_1[...] = load((first, back_a, back_b), every, every)
    back_far_2[...] = load((first, back_b, back_a), every, every)


def far_tiles(sides, relayed_here, *operands, scale):
    kv, part, sums = operands[0], operands[4], operands[7]
    part_done = jax.ShapeDtypeStruct(part.shape, jnp.bfloat16)
    done = jax.ShapeDtypeStruct(kv.shape, jnp.bfloat16)
    sent = jax.ShapeDtypeStruct((kv.shape[0] + PAD, kv.shape[1]), jnp.bfloat16)
    results = pl.pallas_call(
        functools.partial(far_kernel, scale=scale),
        in_specs=[pl.BlockSpec(memory_space=pltpu.SMEM)] * 2 + [WHOLE] * len(operands),
        out_specs=[WHOLE] * 8,
        out_shape=[part_done] * 4 + [done, sent] + [jax.ShapeDtypeStruct(sums.shape, sums.dtype)] * 2,
        scratch_shapes=[pltpu.VMEM(part.shape, part.dtype)] * 2,
        input_output_aliases={9: 6, 10: 7},
        compiler_params=PARAMS,
        name="far_tiles",
    )(sides, relayed_here, *operands)
    return results[:6]


def sum_other_kernel(dq, back_a, back_b, out, *, scale):
    total = dq[...] * scale + back_a[...].astype(jnp.float32) + back_b[...].astype(jnp.float32)
    out[...] = total.astype(jnp.bfloat16)


def sum_other(dq, back_a, back_b, scale):
    return pl.pallas_call(
        functools.partial(sum_other_kernel, scale=scale),
        in_specs=[WHOLE] * 3,
        out_specs=WHOLE,
        out_shape=jax.ShapeDtypeStruct(dq.shape, jnp.bfloat16),
        compiler_params=PARAMS,
        name="sum_other",
    )(dq, back_a, back_b)


def finish_kernel(x_ref, dq_own, back_a, back_b, dkv_own, dkv_other, dq, dk, dv, buffer, sems, *, scale):
    rows, half = buffer.shape
    at_own = pl.ds(pl.multiple_of(x_ref[0] * half, LANES), half)
    at_other = pl.ds(pl.multiple_of((1 - x_ref[0]) * half, LANES), half)
    moves = (
        (dkv_own.at[0:rows], dk.at[:, at_own]),
        (dkv_own.at[rows : 2 * rows], dv.at[:, at_own]),
        (dkv_other.at[0:rows], dk.at[:, at_other]),
        (dkv_other.at[rows : 2 * rows], dv.at[:, at_other]),
    )
    copies = [pltpu.make_async_copy(a, b, sems.at[n]) for n, (a, b) in enumerate(moves)]
    for copy in copies:
        copy.start()
    total = (
        dq_own[...] * scale + back_a[...].astype(jnp.float32) + back_b[...].astype(jnp.float32)
    )
    buffer[...] = total.astype(jnp.bfloat16)
    copies.append(pltpu.make_async_copy(buffer, dq.at[:, at_own], sems.at[4]))
    copies[-1].start()
    for copy in copies:
        copy.wait()


def finish(x, dq_own, back_a, back_b, dkv_own, dkv_other, scale):
    rows, half = dq_own.shape
    return pl.pallas_call(
        functools.partial(finish_kernel, scale=scale),
        in_specs=[pl.BlockSpec(memory_space=pltpu.SMEM)] + [WHOLE] * 5,
        out_specs=[IN_HBM] * 3,
        out_shape=[jax.ShapeDtypeStruct((rows, 2 * half), jnp.bfloat16)] * 3,
        scratch_shapes=[pltpu.VMEM((rows, half), jnp.bfloat16), pltpu.SemaphoreType.DMA((5,))],
        compiler_params=PARAMS,
        name="finish",
    )(x, dq_own, back_a, back_b, dkv_own, dkv_other)


def place_kernel(x_ref, part, _, whole, sem):
    half = part.shape[1]
    at_other = pl.ds(pl.multiple_of((1 - x_ref[0]) * half, LANES), half)
    copy = pltpu.make_async_copy(part, whole.at[:, at_other], sem)
    copy.start()
    copy.wait()


def place(x, part, whole):
    return pl.pallas_call(
        place_kernel,
        in_specs=[pl.BlockSpec(memory_space=pltpu.SMEM), WHOLE, IN_HBM],
        out_specs=IN_HBM,
        out_shape=jax.ShapeDtypeStruct(whole.shape, whole.dtype),
        scratch_shapes=[pltpu.SemaphoreType.DMA],
        input_output_aliases={2: 0},
        compiler_params=PARAMS,
        name="place",
    )(x, part, whole)


def per_device(query_rows, key_rows, value_rows, layer_output, output_grad, log_norms):
    count = lax.axis_size("outer") * lax.axis_size("inner")
    index = lax.axis_index("outer") * lax.axis_size("inner") + lax.axis_index("inner")
    column, row = index % 2, index // 2 % 2
    x = column.astype(jnp.int32).reshape(1)
    sides = (column ^ row).astype(jnp.int32).reshape(1)
    head_size = query_rows.shape[1] // log_norms.shape[0]
    scale = head_size ** (-0.5)

    swap = [(i, i ^ 1) for i in range(count)]
    step_1 = [(i, i ^ 2) for i in range(count)]
    step_2 = [(i, ((i + 2) ^ 2) - 2) for i in range(count)]
    step_2 = [(i, j) for i, j in step_2 if 0 <= j < count]
    half = count // 2
    across = [(half - 2 + k, count - 2 + k) for k in range(2)] + [(half + k, k) for k in range(2)]
    onward = [(count - 2 + k, half + k) for k in range(2)] + [(k, half - 2 + k) for k in range(2)]
    step_2_own = [(i, j) for i, j in step_2 if (i < half) == (j < half)]
    relayed_here = ((index >= half - 2) & (index < half + 2)).astype(jnp.int32).reshape(1)

    def send(a, perm):
        return lax.ppermute(a, AXES, perm)

    (to_other,) = pack(x, query_rows, layer_output, output_grad, log_norms, name="pack_other")
    own, kv_to_other = pack(
        x, query_rows, layer_output, output_grad, log_norms, key_rows, value_rows, name="pack_own"
    )
    other = send(to_other, swap)
    near_1, near_2 = send(own, step_1), send(own, step_2_own)
    relayed = send(send(own, across), onward)
    kv_to_other, other = lax.optimization_barrier((kv_to_other, other))
    kv_other = send(kv_to_other, swap)
    far_1, far_2 = send(other, step_1), send(other, step_2)
    dq_own, dq_other, dq_1, dq_2, dkv, kv_own = near_tiles(
        x, key_rows, value_rows, own, other, near_1, near_2, scale=scale
    )
    dq_own, dq_other, back_near_a, back_near_b, dkv_part = mid_tiles(
        sides, kv_other, own, other, near_1, near_2,
        dq_own, dq_other, dq_1, dq_2, scale=scale,
    )
    near_to_1, near_to_2, far_to_1, far_to_2, dkv_own, dkv_to_other = far_tiles(
        sides, relayed_here, kv_own, kv_other, far_1, far_2, back_near_a, back_near_b, relayed,
        dkv, dkv_part, scale=scale,
    )
    dkv_other = send(dkv_to_other, swap)
    far_back_1, far_back_2 = send(far_to_1, step_1), send(far_to_2, step_2)
    back_1, back_2 = send(near_to_1, step_1), send(near_to_2, step_2)
    dq_from_other = send(sum_other(dq_other, far_back_1, far_back_2, scale), swap)
    dq, dk, dv = finish(x, dq_own, back_1, back_2, dkv_own, dkv_other, scale)
    return place(x, dq_from_other, dq), dk, dv


def solution(mesh):
    rows = P(AXES, None)
    return jax.shard_map(
        per_device,
        mesh=mesh,
        in_specs=(rows, rows, rows, rows, rows, P(None, AXES)),
        out_specs=(rows, rows, rows),
        check_vma=False,
    )
```
